32 devices in a mesh: ctx: 4 (over y, x), head: 8 (over z, core).
Axes of the slice: x: 2, y: 2, z: 4, core: 2. Of those that a mesh axis runs over, the one named last changes fastest.
Arguments:
- queries: bfloat16 [1024, 128, 128], P('ctx', 'head'), may hold values from -24 to 24
- cache_keys: bfloat16 [8, 3072, 128], P(None, 'ctx'), may hold values from -12 to 12
- cache_values: bfloat16 [8, 3072, 128], P(None, 'ctx'), may hold values from -6 to 6
- scale_index: int32 [8, 24], P(None, 'ctx'), may hold values from 0 to 63
- scale_table: float32 [2, 64], replicated, may hold values from 0.6 to 1.6
- hist_lengths: int32 [4], P('ctx'), may hold values from 192 to 768, as said below
- span_offsets: int32 [8], replicated, may hold values from 0 to 3072
- new_keys: bfloat16 [1024, 8, 128], P('ctx'), may hold values from -12 to 12
- new_values: bfloat16 [1024, 8, 128], P('ctx'), may hold values from -6 to 6
- head_groups: int32 [128], P('head'), may hold values from 0 to 7, as said below
- out_weight: bfloat16 [16384, 8192], P('head'), may hold values from -0.5 to 0.5
Outputs:
- projected: bfloat16 [1024, 8192], P('ctx', 'head')
The draws below stay inside these ranges and needn't reach their ends.
Inputs may be any that keep to these rules, and one draw needn't show every extreme that they name: `head_groups`: each key-value head serves exactly 16 query heads. `hist_lengths`: at least one block is full.
All inputs are finite; a program needn't handle non-finite values.
Results may differ from the reference program's by a relative error of at most 0.0058.
Values may be sent and summed in bfloat16 or wider, within the bound.
A program may use at most 128 MiB of HBM per device.

```python
import math
import jax
import jax.numpy as jnp
from jax import lax

H = 128
KVH = 8
DH = 128
D_OUT = 8192
HISTORY_SLOTS = 768
SPAN = 128
SBLK = 128
NSCALE = 64
QROWS = 1024
SPANS = 8
SLOTS = 3072
NBLK = 24
N_CTX = 4


def draw_queries(key, part):
    key = jax.random.fold_in(key, 11)
    values = jax.random.normal(key, (QROWS, H, DH), jnp.float32)
    return jnp.clip(values, -24.0, 24.0).astype(jnp.bfloat16)


def draw_cache_keys(key, part):
    key = jax.random.fold_in(key, 12)
    values = jax.random.normal(key, (KVH, SLOTS, DH), jnp.float32)
    return jnp.clip(values, -12.0, 12.0).astype(jnp.bfloat16)


def draw_new_keys(key, part):
    key = jax.random.fold_in(key, 13)
    values = jax.random.normal(key, (QROWS, KVH, DH), jnp.float32)
    return jnp.clip(values, -12.0, 12.0).astype(jnp.bfloat16)


def draw_hist_lengths(key, part):
    key = jax.random.fold_in(key, 14)
    counts = jax.random.randint(key, (N_CTX,), HISTORY_SLOTS // 4, HISTORY_SLOTS + 1, jnp.int32)
    chosen = jax.random.randint(jax.random.fold_in(key, 1), (), 0, N_CTX, jnp.int32)
    return jnp.where(jnp.arange(N_CTX, dtype=jnp.int32) == chosen, HISTORY_SLOTS, counts).astype(jnp.int32)


def draw_head_groups(key, part):
    key = jax.random.fold_in(key, 15)
    order = jax.random.permutation(key, H)
    return (order // (H // KVH)).astype(jnp.int32)


def plant(result, stream_key, smallest, high):
    index_at = [jax.random.randint(jax.random.fold_in(stream_key, axis), (), 0, length) for axis, length in enumerate(result.shape)]
    main_axis = result.shape.index(max(result.shape))
    neighbour = index_at[:main_axis] + [(index_at[main_axis] + 1) % result.shape[main_axis]] + index_at[main_axis + 1:]
    return result.at[tuple(index_at)].set(smallest).at[tuple(neighbour)].set(high)


def strengthened(values, key, source, target, blocks, factor):
    owner, partner = [(jnp.arange(values.shape[axis_at]) // (values.shape[axis_at] // blocks)).reshape([-1 if axis == axis_at else 1 for axis in range(values.ndim)]) for axis_at in (source, target)]
    chosen = jax.random.permutation(key, blocks)[partner]
    strong = (owner == chosen) | (owner == (partner + blocks // 2) % blocks)
    return jnp.where(strong, factor * values, values)


def shard_levels(stream_key, shape, cuts, least, top_value):
    loudness, own = 1.0, jax.random.fold_in(stream_key, 6)
    for dim, shards_of in cuts:
        steps = jnp.exp(jax.random.uniform(jax.random.fold_in(own, dim), (shards_of,), jnp.float32, least / len(cuts), top_value / len(cuts)))
        loudness = loudness * jnp.repeat(steps, shape[dim] // shards_of).reshape([-1 if axis == dim else 1 for axis in range(len(shape))])
    return loudness


def normal_values(rng, dims, deviation, reach, cuts=(), kind=jnp.bfloat16):
    gain = shard_levels(rng, dims, cuts, -0.22, 0.18) if cuts else 1.0
    values = jax.random.normal(rng, dims, jnp.float32) * deviation * gain
    return jnp.minimum(jnp.maximum(values, -reach), reach).astype(kind)


def heavy_noise(own_key, dims, spread, reach, cuts, heavy, kind=jnp.bfloat16):
    drawn = spread * jax.random.normal(own_key, dims, jnp.float32)
    if cuts:
        drawn = drawn * shard_levels(own_key, dims, cuts, -0.22, 0.18)
    return jnp.clip(strengthened(drawn, jax.random.fold_in(own_key, 3), *heavy), -reach, reach).astype(kind)


def setup_inputs(seed: int = 0) -> dict:
    seeds = jax.random.split(jax.random.key(seed), 12)
    queries = draw_queries(jax.random.fold_in(seeds[11], 71), 0)
    cache_keys = draw_cache_keys(jax.random.fold_in(seeds[11], 71), 0)
    cache_values = normal_values(seeds[2], (KVH, SLOTS, DH), 1.0, 6.0, ((1, 4),))
    scale_index = plant(jax.random.randint(seeds[3], (KVH, NBLK), 0, NSCALE), jax.random.fold_in(seeds[3], 1), 0, NSCALE - 1).astype(jnp.int32)
    scale_table = jnp.clip(jnp.exp(jax.random.uniform(seeds[4], (2, NSCALE), jnp.float32, math.log(0.6), math.log(1.6))), 0.6, 1.6)
    hist_lengths = draw_hist_lengths(jax.random.fold_in(seeds[11], 71), 0)
    span_offsets = plant(jax.random.randint(seeds[6], (SPANS,), 0, SLOTS + 1), jax.random.fold_in(seeds[6], 1), 0, SLOTS).astype(jnp.int32)
    new_keys = draw_new_keys(jax.random.fold_in(seeds[11], 71), 0)
    new_values = normal_values(seeds[8], (QROWS, KVH, DH), 1.0, 6.0, ((0, 4),))
    head_groups = draw_head_groups(jax.random.fold_in(seeds[11], 71), 0)
    out_weight = heavy_noise(seeds[10], (H * DH, D_OUT), (H * DH // 64) ** -0.5, 0.5, ((0, 8),), (0, 1, 8, 2.0))
    return {"queries": queries, "cache_keys": cache_keys, "cache_values": cache_values, "scale_index": scale_index, "scale_table": scale_table, "hist_lengths": hist_lengths, "span_offsets": span_offsets, "new_keys": new_keys, "new_values": new_values, "head_groups": head_groups, "out_weight": out_weight}


floor_score = -1e+30

def reference(queries, cache_keys, cache_values, scale_index, scale_table, hist_lengths, span_offsets, new_keys, new_values, head_groups, out_weight):
    inverse = 1.0 / math.sqrt(DH)
    starts = (jnp.cumsum(hist_lengths) - hist_lengths).astype(jnp.int32)
    per_block_key_scales = jnp.repeat(scale_table[0][scale_index], SBLK, axis=1) * inverse
    value_scales = jnp.repeat(scale_table[1][scale_index], SBLK, axis=1)
    row_limits = jnp.repeat(span_offsets, SPAN)
    slot_ids = jnp.arange(HISTORY_SLOTS, dtype=jnp.int32)
    causal = jnp.arange(SPAN)[:, None] >= jnp.arange(SPAN)[None, :]

    def one_head(head):
        head_group_index = head_groups[head]
        query = queries[:, head, :]
        keys_all = cache_keys[head_group_index]
        values_all = cache_values[head_group_index]
        key_scale_factor = per_block_key_scales[head_group_index]
        vscale = value_scales[head_group_index]
        parts = []
        lses = []
        for block in range(N_CTX):
            leading_entry = block * HISTORY_SLOTS
            unscaled_scores = jnp.dot(query, keys_all[leading_entry:leading_entry + HISTORY_SLOTS].T, preferred_element_type=jnp.float32)
            logit_scores = unscaled_scores * key_scale_factor[leading_entry:leading_entry + HISTORY_SLOTS]
            live = slot_ids < hist_lengths[block]
            visible = live[None, :] & ((starts[block] + slot_ids)[None, :] < row_limits[:, None])
            masked = jnp.where(visible, logit_scores, floor_score)
            block_top = lax.optimization_barrier(jnp.max(masked, axis=1))
            block_expo = jnp.where(visible, jnp.exp(masked - block_top[:, None]), 0.0)
            any_visible = jnp.any(visible, axis=1)
            block_total = jnp.where(any_visible, lax.optimization_barrier(jnp.sum(block_expo, axis=1)), 1.0)
            weights = (block_expo * vscale[leading_entry:leading_entry + HISTORY_SLOTS]).astype(jnp.bfloat16)
            mixed = jnp.dot(weights, values_all[leading_entry:leading_entry + HISTORY_SLOTS], preferred_element_type=jnp.float32) / block_total[:, None]
            parts.append(mixed.astype(jnp.bfloat16))
            lses.append(jnp.where(any_visible, block_top + jnp.log(block_total), floor_score))
        query_spans = query.reshape(SPANS, SPAN, DH).astype(jnp.float32)
        key_spans = new_keys[:, head_group_index, :].reshape(SPANS, SPAN, DH).astype(jnp.float32)
        value_spans = new_values[:, head_group_index, :].reshape(SPANS, SPAN, DH).astype(jnp.float32)
        fresh_raw = jnp.einsum('crd,csd->crs', query_spans, key_spans) * inverse
        fresh_masked = jnp.where(causal[None], fresh_raw, floor_score)
        fresh_top = lax.optimization_barrier(jnp.max(fresh_masked, axis=2))
        fresh_expo = jnp.where(causal[None], jnp.exp(fresh_masked - fresh_top[:, :, None]), 0.0)
        fresh_total = lax.optimization_barrier(jnp.sum(fresh_expo, axis=2))
        fresh_weights = fresh_expo.astype(jnp.bfloat16).astype(jnp.float32)
        fresh = jnp.einsum('crs,csd->crd', fresh_weights, value_spans) / fresh_total[:, :, None]
        fresh = fresh.reshape(QROWS, DH)
        fresh_lse = (fresh_top + jnp.log(fresh_total)).reshape(QROWS)
        stacked = jnp.stack(lses)
        peak = jnp.maximum(lax.optimization_barrier(jnp.max(stacked, axis=0)), fresh_lse)
        block_weight = jnp.exp(stacked - peak[None, :])
        fresh_weight = jnp.exp(fresh_lse - peak)
        numer = fresh_weight[:, None] * fresh + lax.optimization_barrier(jnp.sum(block_weight[:, :, None] * jnp.stack(parts).astype(jnp.float32), axis=0))
        denom = fresh_weight + lax.optimization_barrier(jnp.sum(block_weight, axis=0))
        return (numer / denom[:, None]).astype(jnp.bfloat16)
    attended = lax.map(one_head, jnp.arange(H, dtype=jnp.int32))
    flat = jnp.transpose(attended, (1, 0, 2)).reshape(QROWS, H * DH)
    return jnp.dot(flat, out_weight, preferred_element_type=jnp.float32).astype(jnp.bfloat16)
```

```python
import math

import jax
import jax.numpy as jnp
from jax import lax
from jax.experimental import pallas as pl
from jax.experimental.pallas import tpu as pltpu
from jax.sharding import PartitionSpec as P

MESH = pl.DeviceIdType.MESH

SPAN = 128


floor_score = -1e30


def entering(part, axis, combine, identity):
    place = lax.axis_index(axis)
    gathered = lax.all_gather(part, axis)
    state = jnp.zeros_like(part) + jnp.asarray(identity, part.dtype)

    def one(hop, state):
        return combine(state, lax.dynamic_index_in_dim(gathered, hop, 0, False))

    return lax.fori_loop(0, place, one, state)


def passed_along(value, axis, steps):
    count = lax.axis_size(axis)
    pairs = [(source, (source + steps) % count) for source in range(count)]
    return lax.ppermute(value, axis, pairs)


def add_counts(earlier, later):
    return earlier + later


def project_and_reduce(flat, out_weight):
    heads = lax.axis_size("head")
    planes = heads // 2
    rows, depth = flat.shape
    width = out_weight.shape[1] // heads
    pieces = 4
    piece = rows // pieces
    tile = 256
    slots = 4
    order = [
        sorted(range(planes), key=lambda d, z=z: (-abs(d - z), -d if z < planes // 2 else d))
        for z in range(planes)
    ]

    def kernel(
        flat_ref, weight_ref, out_ref, weights, own, pair_out, pair_in,
        up_out, up_in, down_out, down_in,
        weight_sem, pair_send, pair_recv, up_send, up_recv, down_send, down_recv,
    ):
        me = lax.axis_index("head")
        plane = me // 2
        core = me % 2
        sibling = {"head": 2 * plane + 1 - core}
        above = {"head": me + 2}
        below = {"head": me - 2}
        has_above = plane < planes - 1
        has_below = plane > 0

        def target(step):
            d = jnp.int32(order[0][step])
            for z in range(1, planes):
                d = jnp.where(plane == z, order[z][step], d)
            return d

        targets = [target(step) for step in range(planes)]
        blocks = []
        for d in targets:
            blocks += [2 * d + 1 - core, 2 * d + core]

        def fetch(i):
            column = pl.multiple_of(blocks[i] * width, width)
            return pltpu.make_async_copy(
                weight_ref.at[:, pl.ds(column, width)], weights.at[i % slots], weight_sem.at[i % slots]
            )

        for i in range(slots - 1):
            fetch(i).start()

        barrier = pltpu.get_barrier_semaphore()
        pl.semaphore_signal(barrier, inc=1, device_id=sibling, device_id_type=MESH)

        @pl.when(has_above)
        def _():
            pl.semaphore_signal(barrier, inc=1, device_id=above, device_id_type=MESH)

        @pl.when(has_below)
        def _():
            pl.semaphore_signal(barrier, inc=1, device_id=below, device_id_type=MESH)

        pl.semaphore_wait(barrier, 1 + has_above.astype(jnp.int32) + has_below.astype(jnp.int32))

        def to_sibling(d):
            return pltpu.make_async_remote_copy(
                src_ref=pair_out.at[d], dst_ref=pair_in.at[d],
                send_sem=pair_send.at[d], recv_sem=pair_recv.at[d],
                device_id=sibling, device_id_type=MESH,
            )

        def upward(d, p):
            return pltpu.make_async_remote_copy(
                src_ref=up_out.at[d, p], dst_ref=up_in.at[d, p],
                send_sem=up_send.at[d, p], recv_sem=up_recv.at[d, p],
                device_id=above, device_id_type=MESH,
            )

        def downward(d, p):
            return pltpu.make_async_remote_copy(
                src_ref=down_out.at[d, p], dst_ref=down_in.at[d, p],
                send_sem=down_send.at[d, p], recv_sem=down_recv.at[d, p],
                device_id=below, device_id_type=MESH,
            )

        def multiply(i, store):
            if i + slots - 1 < len(blocks):
                fetch(i + slots - 1).start()
            fetch(i).wait()

            @pl.loop(0, width // tile)
            def _(t):
                columns = pl.ds(pl.multiple_of(t * tile, tile), tile)
                store(
                    columns,
                    jnp.dot(
                        flat_ref[...], weights[i % slots, :, columns],
                        preferred_element_type=jnp.float32,
                    ),
                )

        def combine(d):
            to_sibling(d).wait_recv()

            @pl.loop(0, pieces)
            def _(p):
                span = pl.ds(pl.multiple_of(p * piece, piece), piece)

                @pl.when(d > plane)
                def _():
                    total = own[d, span] + pair_in[d, span].astype(jnp.float32)

                    @pl.when(has_below)
                    def _():
                        upward(d, p).wait_recv()
                        up_out[d, p] = (total + up_in[d, p].astype(jnp.float32)).astype(jnp.bfloat16)

                    @pl.when(jnp.logical_not(has_below))
                    def _():
                        up_out[d, p] = total.astype(jnp.bfloat16)

                    upward(d, p).start()

                @pl.when(d < plane)
                def _():
                    total = own[d, span] + pair_in[d, span].astype(jnp.float32)

                    @pl.when(has_above)
                    def _():
                        downward(d, p).wait_recv()
                        down_out[d, p] = (total + down_in[d, p].astype(jnp.float32)).astype(
                            jnp.bfloat16
                        )

                    @pl.when(jnp.logical_not(has_above))
                    def _():
                        down_out[d, p] = total.astype(jnp.bfloat16)

                    downward(d, p).start()

                @pl.when(d == plane)
                def _():
                    own[d, span] = own[d, span] + pair_in[d, span].astype(jnp.float32)

                    @pl.when(has_below)
                    def _():
                        upward(d, p).wait_recv()
                        own[d, span] = own[d, span] + up_in[d, p].astype(jnp.float32)

                    @pl.when(has_above)
                    def _():
                        downward(d, p).wait_recv()
                        own[d, span] = own[d, span] + down_in[d, p].astype(jnp.float32)

                    out_ref[span] = own[d, span].astype(jnp.bfloat16)

        for step in range(planes):
            d = targets[step]

            def to_pair(columns, value, d=d):
                pair_out[d, :, columns] = value.astype(jnp.bfloat16)

            def to_own(columns, value, d=d):
                own[d, :, columns] = value

            multiply(2 * step, to_pair)
            to_sibling(d).start()
            multiply(2 * step + 1, to_own)
            if step > 0:
                combine(targets[step - 1])
        combine(targets[planes - 1])

        for step in range(planes):
            d = targets[step]
            to_sibling(d).wait_send()

            @pl.loop(0, pieces)
            def _(p, d=d):
                @pl.when(d > plane)
                def _():
                    upward(d, p).wait_send()

                @pl.when(d < plane)
                def _():
                    downward(d, p).wait_send()

    block = (planes, rows, width)
    cut = (planes, pieces, piece, width)
    dma = pltpu.SemaphoreType.DMA
    return pl.pallas_call(
        kernel,
        out_shape=jax.ShapeDtypeStruct((rows, width), jnp.bfloat16),
        in_specs=[pl.BlockSpec(memory_space=pltpu.VMEM), pl.BlockSpec(memory_space=pl.ANY)],
        out_specs=pl.BlockSpec(memory_space=pltpu.VMEM),
        scratch_shapes=[
            pltpu.VMEM((slots, depth, width), jnp.bfloat16),
            pltpu.VMEM(block, jnp.float32),
            pltpu.VMEM(block, jnp.bfloat16),
            pltpu.VMEM(block, jnp.bfloat16),
            pltpu.VMEM(cut, jnp.bfloat16),
            pltpu.VMEM(cut, jnp.bfloat16),
            pltpu.VMEM(cut, jnp.bfloat16),
            pltpu.VMEM(cut, jnp.bfloat16),
            dma((slots,)),
            dma((planes,)),
            dma((planes,)),
            dma((planes, pieces)),
            dma((planes, pieces)),
            dma((planes, pieces)),
            dma((planes, pieces)),
        ],
        compiler_params=pltpu.CompilerParams(
            collective_id=1, has_side_effects=True, vmem_limit_bytes=56 * 1024 * 1024
        ),
        cost_estimate=pl.CostEstimate(
            flops=2 * rows * depth * width * heads,
            bytes_accessed=2 * depth * width * heads,
            transcendentals=0,
        ),
        name="project_and_reduce",
    )(flat, out_weight)


def shards(
    queries,
    cache_keys,
    cache_values,
    scale_index,
    scale_table,
    hist_lengths,
    span_offsets,
    new_keys,
    new_values,
    head_groups,
    out_weight,
):
    ctx_count = lax.axis_size("ctx")
    position_me = lax.axis_index("ctx")
    row_count, heads_here, head_width = queries.shape
    slot_count = cache_keys.shape[1]
    spans_here = row_count // SPAN
    inverse = 1.0 / math.sqrt(head_width)
    codes = jnp.arange(scale_table.shape[1], dtype=jnp.int32)
    one_hot = (scale_index[:, :, None] == codes[None, None, :]).astype(jnp.float32)
    block_scales = jnp.einsum("kbn,tn->tkb", one_hot, scale_table, precision=lax.Precision.HIGHEST)
    slot_scales = jnp.repeat(block_scales, slot_count // scale_index.shape[1], axis=2)
    head_scales = jnp.take(slot_scales, head_groups, axis=1)
    per_block_key_scales = head_scales[0] * inverse
    value_scales = head_scales[1]
    keys_here = jnp.take(cache_keys, head_groups, axis=0)
    values_here = jnp.take(cache_values, head_groups, axis=0)
    start_slot = entering(hist_lengths, "ctx", add_counts, jnp.zeros_like(hist_lengths))
    slot_ids = jnp.arange(slot_count, dtype=jnp.int32)
    live = slot_ids < hist_lengths[0]
    positions = start_slot[0] + slot_ids

    def block_partial(query_block, source):
        offsets = lax.dynamic_slice_in_dim(span_offsets, source * spans_here, spans_here)
        limits = jnp.repeat(offsets, SPAN)
        visible = live[None, :] & (positions[None, :] < limits[:, None])
        unscaled_scores = jnp.einsum(
            "rhd,hsd->hrs", query_block, keys_here, preferred_element_type=jnp.float32
        )
        logit_scores = unscaled_scores * per_block_key_scales[:, None, :]
        masked = jnp.where(visible[None], logit_scores, floor_score)
        block_top = jnp.max(masked, axis=2)
        block_expo = jnp.where(visible[None], jnp.exp(masked - block_top[:, :, None]), 0.0)
        any_visible = jnp.any(visible, axis=1)
        block_total = jnp.where(any_visible[None, :], jnp.sum(block_expo, axis=2), 1.0)
        weights = (block_expo * value_scales[:, None, :]).astype(jnp.bfloat16)
        mixed = jnp.einsum("hrs,hsd->rhd", weights, values_here, preferred_element_type=jnp.float32)
        mixed = mixed / jnp.transpose(block_total)[:, :, None]
        block_lse = jnp.where(any_visible[None, :], block_top + jnp.log(block_total), floor_score)
        return (mixed.astype(jnp.bfloat16), block_lse)

    def record(parts, lses, source, query_block):
        part, block_lse = block_partial(query_block, source)
        parts = lax.dynamic_update_index_in_dim(parts, part, source, 0)
        lses = lax.dynamic_update_index_in_dim(lses, block_lse, source, 0)
        return (parts, lses)

    def forward(query_block):
        return passed_along(query_block, "ctx", 1)

    parts = jnp.zeros((ctx_count, row_count, heads_here, head_width), jnp.bfloat16)
    lses = jnp.full((ctx_count, heads_here, row_count), floor_score, jnp.float32)
    parts, lses = record(parts, lses, position_me, queries)

    def one_turn(turn, carry):
        travelling, parts_now, lses_now = carry
        travelling = forward(travelling)
        parts_now, lses_now = record(
            parts_now, lses_now, (position_me - turn) % ctx_count, travelling
        )
        return (travelling, parts_now, lses_now)

    travelling, parts, lses = lax.fori_loop(1, ctx_count, one_turn, (queries, parts, lses))
    query_spans = queries.reshape(spans_here, SPAN, heads_here, head_width)
    fresh_keys = jnp.take(new_keys, head_groups, axis=1).reshape(
        spans_here, SPAN, heads_here, head_width
    )
    fresh_values = jnp.take(new_values, head_groups, axis=1).reshape(
        spans_here, SPAN, heads_here, head_width
    )
    causal = jnp.arange(SPAN)[:, None] >= jnp.arange(SPAN)[None, :]
    fresh_raw = (
        jnp.einsum("crhd,cshd->chrs", query_spans, fresh_keys, preferred_element_type=jnp.float32)
        * inverse
    )
    fresh_masked = jnp.where(causal[None, None], fresh_raw, floor_score)
    fresh_top = jnp.max(fresh_masked, axis=3)
    fresh_expo = jnp.where(causal[None, None], jnp.exp(fresh_masked - fresh_top[..., None]), 0.0)
    fresh_total = jnp.sum(fresh_expo, axis=3)
    fresh_weights = fresh_expo.astype(jnp.bfloat16)
    fresh = jnp.einsum(
        "chrs,cshd->crhd", fresh_weights, fresh_values, preferred_element_type=jnp.float32
    )
    fresh = fresh / jnp.transpose(fresh_total, (0, 2, 1))[..., None]
    fresh = fresh.reshape(row_count, heads_here, head_width)
    fresh_lse = jnp.transpose(fresh_top + jnp.log(fresh_total), (1, 0, 2)).reshape(
        heads_here, row_count
    )
    home_parts, home_lses = (
        lax.all_to_all(parts.astype(jnp.float32), "ctx", split_axis=0, concat_axis=0, tiled=True),
        lax.all_to_all(lses, "ctx", split_axis=0, concat_axis=0, tiled=True),
    )
    peak = jnp.maximum(jnp.max(home_lses, axis=0), fresh_lse)
    block_weight = jnp.exp(home_lses - peak[None])
    fresh_weight = jnp.exp(fresh_lse - peak)
    numer_all = jnp.transpose(fresh_weight)[:, :, None] * fresh
    numer_all = numer_all + jnp.sum(
        jnp.transpose(block_weight, (0, 2, 1))[..., None] * home_parts, axis=0
    )
    denom_all = fresh_weight + jnp.sum(block_weight, axis=0)
    attended = (numer_all / jnp.transpose(denom_all)[:, :, None]).astype(jnp.bfloat16)
    flat = attended.reshape(row_count, heads_here * head_width)
    return project_and_reduce(flat, out_weight)


def solution(mesh):
    placed = (
        P("ctx", "head", None),
        P(None, "ctx", None),
        P(None, "ctx", None),
        P(None, "ctx"),
        P(),
        P("ctx"),
        P(),
        P("ctx", None, None),
        P("ctx", None, None),
        P("head"),
        P("head", None),
    )
    return jax.shard_map(
        shards, mesh=mesh, in_specs=placed, out_specs=P("ctx", "head"), check_vma=False
    )
```

```python
import math

import jax
import jax.numpy as jnp
from jax import lax
from jax.experimental import pallas as pl
from jax.experimental.pallas import tpu as pltpu
from jax.sharding import PartitionSpec as P

MESH = pl.DeviceIdType.MESH
LOG2E = math.log2(math.e)

SPAN = 128


floor_score = -1e30


def entering(part, axis, combine, identity):
    place = lax.axis_index(axis)
    gathered = lax.all_gather(part, axis)
    state = jnp.zeros_like(part) + jnp.asarray(identity, part.dtype)

    def one(hop, state):
        return combine(state, lax.dynamic_index_in_dim(gathered, hop, 0, False))

    return lax.fori_loop(0, place, one, state)


def passed_along(value, axis, steps):
    count = lax.axis_size(axis)
    pairs = [(source, (source + steps) % count) for source in range(count)]
    return lax.ppermute(value, axis, pairs)


def add_counts(earlier, later):
    return earlier + later


def project_and_reduce(flat, out_weight):
    heads = lax.axis_size("head")
    planes = heads // 2
    rows, depth = flat.shape
    width = out_weight.shape[1] // heads
    pieces = 4
    piece = rows // pieces
    tile = 256
    slots = 4
    order = [
        sorted(range(planes), key=lambda d, z=z: (-abs(d - z), -d if z < planes // 2 else d))
        for z in range(planes)
    ]

    def kernel(
        flat_ref, weight_ref, out_ref, weights, own, pair_out, pair_in,
        up_out, up_in, down_out, down_in,
        weight_sem, pair_send, pair_recv, up_send, up_recv, down_send, down_recv,
    ):
        me = lax.axis_index("head")
        plane = me // 2
        core = me % 2
        sibling = {"head": 2 * plane + 1 - core}
        above = {"head": me + 2}
        below = {"head": me - 2}
        has_above = plane < planes - 1
        has_below = plane > 0

        def target(step):
            d = jnp.int32(order[0][step])
            for z in range(1, planes):
                d = jnp.where(plane == z, order[z][step], d)
            return d

        targets = [target(step) for step in range(planes)]
        blocks = []
        for d in targets:
            blocks += [2 * d + 1 - core, 2 * d + core]

        def fetch(i):
            column = pl.multiple_of(blocks[i] * width, width)
            return pltpu.make_async_copy(
                weight_ref.at[:, pl.ds(column, width)], weights.at[i % slots], weight_sem.at[i % slots]
            )

        for i in range(slots - 1):
            fetch(i).start()

        barrier = pltpu.get_barrier_semaphore()
        pl.semaphore_signal(barrier, inc=1, device_id=sibling, device_id_type=MESH)

        @pl.when(has_above)
        def _():
            pl.semaphore_signal(barrier, inc=1, device_id=above, device_id_type=MESH)

        @pl.when(has_below)
        def _():
            pl.semaphore_signal(barrier, inc=1, device_id=below, device_id_type=MESH)

        pl.semaphore_wait(barrier, 1 + has_above.astype(jnp.int32) + has_below.astype(jnp.int32))

        def to_sibling(d):
            return pltpu.make_async_remote_copy(
                src_ref=pair_out.at[d], dst_ref=pair_in.at[d],
                send_sem=pair_send.at[d], recv_sem=pair_recv.at[d],
                device_id=sibling, device_id_type=MESH,
            )

        def upward(d, p):
            return pltpu.make_async_remote_copy(
                src_ref=up_out.at[d, p], dst_ref=up_in.at[d, p],
                send_sem=up_send.at[d, p], recv_sem=up_recv.at[d, p],
                device_id=above, device_id_type=MESH,
            )

        def downward(d, p):
            return pltpu.make_async_remote_copy(
                src_ref=down_out.at[d, p], dst_ref=down_in.at[d, p],
                send_sem=down_send.at[d, p], recv_sem=down_recv.at[d, p],
                device_id=below, device_id_type=MESH,
            )

        def multiply(i, store):
            if i + slots - 1 < len(blocks):
                fetch(i + slots - 1).start()
            fetch(i).wait()

            @pl.loop(0, width // tile)
            def _(t):
                columns = pl.ds(pl.multiple_of(t * tile, tile), tile)
                store(
                    columns,
                    jnp.dot(
                        flat_ref[...], weights[i % slots, :, columns],
                        preferred_element_type=jnp.float32,
                    ),
                )

        def combine(d):
            to_sibling(d).wait_recv()

            @pl.loop(0, pieces)
            def _(p):
                span = pl.ds(pl.multiple_of(p * piece, piece), piece)

                @pl.when(d > plane)
                def _():
                    total = own[d, span] + pair_in[d, span].astype(jnp.float32)

                    @pl.when(has_below)
                    def _():
                        upward(d, p).wait_recv()
                        up_out[d, p] = (total + up_in[d, p].astype(jnp.float32)).astype(jnp.bfloat16)

                    @pl.when(jnp.logical_not(has_below))
                    def _():
                        up_out[d, p] = total.astype(jnp.bfloat16)

                    upward(d, p).start()

                @pl.when(d < plane)
                def _():
                    total = own[d, span] + pair_in[d, span].astype(jnp.float32)

                    @pl.when(has_above)
                    def _():
                        downward(d, p).wait_recv()
                        down_out[d, p] = (total + down_in[d, p].astype(jnp.float32)).astype(
                            jnp.bfloat16
                        )

                    @pl.when(jnp.logical_not(has_above))
                    def _():
                        down_out[d, p] = total.astype(jnp.bfloat16)

                    downward(d, p).start()

                @pl.when(d == plane)
                def _():
                    own[d, span] = own[d, span] + pair_in[d, span].astype(jnp.float32)

                    @pl.when(has_below)
                    def _():
                        upward(d, p).wait_recv()
                        own[d, span] = own[d, span] + up_in[d, p].astype(jnp.float32)

                    @pl.when(has_above)
                    def _():
                        downward(d, p).wait_recv()
                        own[d, span] = own[d, span] + down_in[d, p].astype(jnp.float32)

                    out_ref[span] = own[d, span].astype(jnp.bfloat16)

        for step in range(planes):
            d = targets[step]

            def to_pair(columns, value, d=d):
                pair_out[d, :, columns] = value.astype(jnp.bfloat16)

            def to_own(columns, value, d=d):
                own[d, :, columns] = value

            multiply(2 * step, to_pair)
            to_sibling(d).start()
            multiply(2 * step + 1, to_own)
            if step > 0:
                combine(targets[step - 1])
        combine(targets[planes - 1])

        for step in range(planes):
            d = targets[step]
            to_sibling(d).wait_send()

            @pl.loop(0, pieces)
            def _(p, d=d):
                @pl.when(d > plane)
                def _():
                    upward(d, p).wait_send()

                @pl.when(d < plane)
                def _():
                    downward(d, p).wait_send()

    block = (planes, rows, width)
    cut = (planes, pieces, piece, width)
    dma = pltpu.SemaphoreType.DMA
    return pl.pallas_call(
        kernel,
        out_shape=jax.ShapeDtypeStruct((rows, width), jnp.bfloat16),
        in_specs=[pl.BlockSpec(memory_space=pltpu.VMEM), pl.BlockSpec(memory_space=pl.ANY)],
        out_specs=pl.BlockSpec(memory_space=pltpu.VMEM),
        scratch_shapes=[
            pltpu.VMEM((slots, depth, width), jnp.bfloat16),
            pltpu.VMEM(block, jnp.float32),
            pltpu.VMEM(block, jnp.bfloat16),
            pltpu.VMEM(block, jnp.bfloat16),
            pltpu.VMEM(cut, jnp.bfloat16),
            pltpu.VMEM(cut, jnp.bfloat16),
            pltpu.VMEM(cut, jnp.bfloat16),
            pltpu.VMEM(cut, jnp.bfloat16),
            dma((slots,)),
            dma((planes,)),
            dma((planes,)),
            dma((planes, pieces)),
            dma((planes, pieces)),
            dma((planes, pieces)),
            dma((planes, pieces)),
        ],
        compiler_params=pltpu.CompilerParams(
            collective_id=1, has_side_effects=True, vmem_limit_bytes=56 * 1024 * 1024
        ),
        cost_estimate=pl.CostEstimate(
            flops=2 * rows * depth * width * heads,
            bytes_accessed=2 * depth * width * heads,
            transcendentals=0,
        ),
        name="project_and_reduce",
    )(flat, out_weight)


def gather_and_attend(queries, keys, values, meta, offsets, groups, fresh_keys, fresh_values):
    heads_here, row_count, head_width = queries.shape
    group_count, slot_count, _ = keys.shape
    half = slot_count // 2
    near = group_count // 2
    spans_here = row_count // SPAN
    factor = LOG2E / math.sqrt(head_width)

    def kernel(
        offsets_ref, groups_ref, q_ref, k_ref, v_ref, meta_ref, fk_ref, fv_ref, out_ref,
        xf_k, xf_v, xs_k, xs_v, yf_k, yf_v, ys_k, ys_v, dn_k, dn_v, df_k, df_v,
        meta_x, meta_y, meta_d, bias, top, total, mixed,
        send, recv, meta_send, meta_recv,
    ):
        me = lax.axis_index("ctx")
        head = lax.axis_index("head")
        plane = head // 2
        core = head % 2
        parity = plane % 2
        x_place = me + 1 - 2 * (me % 2)
        y_place = (me + 2) % 4
        d_place = 3 - me
        to_x, to_y, to_d = {"ctx": x_place}, {"ctx": y_place}, {"ctx": d_place}
        sibling = {"head": 2 * plane + 1 - core}
        partner = {"head": head + 2 - 4 * parity}
        barrier = pltpu.get_barrier_semaphore()
        for device in (to_x, to_y, to_d, sibling, partner):
            pl.semaphore_signal(barrier, inc=1, device_id=device, device_id_type=MESH)
        pl.semaphore_wait(barrier, 5)

        mine = pl.ds(core * near, near)
        low = pl.ds(core * near, near // 2)
        high = pl.ds(core * near + near // 2, near // 2)
        first = pl.multiple_of(parity * half, 128)
        second = pl.multiple_of((1 - parity) * half, 128)
        started = []

        def copy(source, target, device):
            i = len(started)
            made = pltpu.make_async_remote_copy(
                src_ref=source, dst_ref=target, send_sem=send.at[i], recv_sem=recv.at[i],
                device_id=device, device_id_type=MESH,
            )
            made.start()
            started.append(made)
            return made

        meta_copies = []
        for i, (target, device) in enumerate(((meta_x, to_x), (meta_y, to_y), (meta_d, to_d))):
            made = pltpu.make_async_remote_copy(
                src_ref=meta_ref, dst_ref=target, send_sem=meta_send.at[i], recv_sem=meta_recv.at[i],
                device_id=device, device_id_type=MESH,
            )
            made.start()
            meta_copies.append(made)

        def own(ref, offset):
            return ref.at[mine, pl.ds(offset, half)]

        firsts = [
            copy(own(ref, first), target.at[mine], device)
            for ref, tx, ty in ((k_ref, xf_k, yf_k), (v_ref, xf_v, yf_v))
            for target, device in ((tx, to_x), (ty, to_y))
        ]

        def fresh_head(h, carry):
            g = groups_ref[h]
            for t in range(spans_here):
                span = pl.ds(t * SPAN, SPAN)
                scores = lax.dot_general(
                    q_ref[h, span], fk_ref[g, span], (((1,), (1,)), ((), ())),
                    preferred_element_type=jnp.float32,
                ) * factor
                causal = lax.broadcasted_iota(jnp.int32, scores.shape, 0) >= lax.broadcasted_iota(
                    jnp.int32, scores.shape, 1
                )
                scores = jnp.where(causal, scores, floor_score)
                largest = jnp.max(scores, axis=1, keepdims=True)
                expo = jnp.exp2(scores - largest)
                top[h, span] = largest
                total[h, span] = jnp.sum(expo, axis=1, keepdims=True)
                mixed[h, span] = jnp.dot(
                    expo.astype(jnp.bfloat16), fv_ref[g, span], preferred_element_type=jnp.float32
                )
            return carry

        lax.fori_loop(0, heads_here, fresh_head, 0, unroll=2)
        for made in meta_copies:
            made.wait_recv()

        places = ((me, meta_ref), (x_place, meta_x), (y_place, meta_y), (d_place, meta_d))
        slot_ids = lax.broadcasted_iota(jnp.int32, (1, slot_count), 1)
        lengths = [m[pl.ds(2 * group_count, 1), :].astype(jnp.int32) for _, m in places]
        for b, (place, _) in enumerate(places):
            start = jnp.zeros((1, slot_count), jnp.int32)
            for (other, _), length in zip(places, lengths):
                start = start + jnp.where(other < place, length, 0)
            for t in range(spans_here):
                limit = offsets_ref[me * spans_here + t]
                visible = (slot_ids < lengths[b]) & (start + slot_ids < limit)
                bias[b, pl.ds(t, 1), :] = jnp.where(visible, 0.0, floor_score)

        def attend(b, offset, size, keys_of, values_of):
            slots = pl.ds(offset, size)
            meta_of = places[b][1]

            def one(h, carry):
                g = groups_ref[h]
                key_rows, value_rows = keys_of(g), values_of(g)
                key_scale = meta_of[pl.ds(g, 1), slots]
                value_scale = meta_of[pl.ds(g + group_count, 1), slots]
                raw = lax.dot_general(
                    q_ref[h], key_rows, (((1,), (1,)), ((), ())), preferred_element_type=jnp.float32
                )
                for t in range(spans_here):
                    span = pl.ds(t * SPAN, SPAN)
                    scores = raw[t * SPAN:(t + 1) * SPAN] * key_scale + bias[b, pl.ds(t, 1), slots]
                    before = top[h, span]
                    largest = jnp.maximum(before, jnp.max(scores, axis=1, keepdims=True))
                    keep = jnp.exp2(before - largest)
                    expo = jnp.exp2(scores - largest)
                    top[h, span] = largest
                    total[h, span] = total[h, span] * keep + jnp.sum(expo, axis=1, keepdims=True)
                    weights = (expo * value_scale).astype(jnp.bfloat16)
                    mixed[h, span] = mixed[h, span] * keep + jnp.dot(
                        weights, value_rows, preferred_element_type=jnp.float32
                    )
                return carry

            lax.fori_loop(0, heads_here, one, 0, unroll=2)

        def attend_ref(b, offset, k, v):
            attend(b, offset, half, lambda g: k[g], lambda g: v[g])

        attend(0, 0, slot_count, lambda g: k_ref[g], lambda g: v_ref[g])

        def share(pairs):
            return [copy(ref.at[part], ref.at[part], sibling) for ref, part in pairs]

        def arrived(copies):
            for made in copies:
                made.wait_recv()

        arrived(firsts)
        relays = [
            copy(source.at[part], target.at[part], device)
            for source, target, part, device in (
                (xf_k, dn_k, low, to_y), (yf_k, dn_k, high, to_x),
                (xf_v, dn_v, low, to_y), (yf_v, dn_v, high, to_x),
            )
        ]
        seconds = [
            copy(own(ref, second), target.at[mine], device)
            for ref, tx, ty in ((k_ref, xs_k, ys_k), (v_ref, xs_v, ys_v))
            for target, device in ((tx, to_x), (ty, to_y))
        ]
        arrived(share([(xf_k, mine), (xf_v, mine), (yf_k, mine), (yf_v, mine)]))
        attend_ref(1, first, xf_k, xf_v)
        arrived(relays)
        across = [
            copy(source.at[part], target.at[part], partner)
            for source, target in ((dn_k, df_k), (dn_v, df_v))
            for part in (low, high)
        ]
        near_shared = share([(dn_k, mine), (dn_v, mine)])
        attend_ref(2, first, yf_k, yf_v)
        arrived(near_shared)
        attend_ref(3, first, dn_k, dn_v)
        arrived(seconds)
        second_shared = share([(xs_k, mine), (xs_v, mine), (ys_k, mine), (ys_v, mine)])
        arrived(across)
        far_shared = share([(df_k, mine), (df_v, mine)])
        arrived(second_shared)
        attend_ref(1, second, xs_k, xs_v)
        attend_ref(2, second, ys_k, ys_v)
        arrived(far_shared)
        attend_ref(3, second, df_k, df_v)

        def finish(h, carry):
            columns = pl.ds(pl.multiple_of(h * head_width, head_width), head_width)
            out_ref[:, columns] = (mixed[h] / total[h]).astype(jnp.bfloat16)
            return carry

        lax.fori_loop(0, heads_here, finish, 0)
        for made in started + meta_copies:
            made.wait_send()

    chunk = pltpu.VMEM((group_count, half, head_width), jnp.bfloat16)
    table = pltpu.VMEM(meta.shape, jnp.float32)
    dma = pltpu.SemaphoreType.DMA
    copies = 4 + 4 + 4 + 4 + 4 + 2 + 4 + 2
    whole = pl.BlockSpec(memory_space=pltpu.VMEM)
    scalar = pl.BlockSpec(memory_space=pltpu.SMEM)
    return pl.pallas_call(
        kernel,
        out_shape=jax.ShapeDtypeStruct((row_count, heads_here * head_width), jnp.bfloat16),
        in_specs=[scalar, scalar] + [whole] * 6,
        out_specs=whole,
        scratch_shapes=[chunk] * 12
        + [table] * 3
        + [
            pltpu.VMEM((4, 8, slot_count), jnp.float32),
            pltpu.VMEM((heads_here, row_count, 1), jnp.float32),
            pltpu.VMEM((heads_here, row_count, 1), jnp.float32),
            pltpu.VMEM((heads_here, row_count, head_width), jnp.float32),
            dma((copies,)),
            dma((copies,)),
            dma((3,)),
            dma((3,)),
        ],
        compiler_params=pltpu.CompilerParams(
            collective_id=2, has_side_effects=True, vmem_limit_bytes=56 * 1024 * 1024
        ),
        cost_estimate=pl.CostEstimate(
            flops=16 * row_count * heads_here * slot_count * head_width,
            bytes_accessed=8 * group_count * slot_count * head_width,
            transcendentals=4 * row_count * heads_here * slot_count,
        ),
        name="gather_and_attend",
    )(offsets, groups, queries, keys, values, meta, fresh_keys, fresh_values)


def shards(
    queries,
    cache_keys,
    cache_values,
    scale_index,
    scale_table,
    hist_lengths,
    span_offsets,
    new_keys,
    new_values,
    head_groups,
    out_weight,
):
    ctx_count = lax.axis_size("ctx")
    position_me = lax.axis_index("ctx")
    row_count, heads_here, head_width = queries.shape
    slot_count = cache_keys.shape[1]
    spans_here = row_count // SPAN
    inverse = 1.0 / math.sqrt(head_width)
    codes = jnp.arange(scale_table.shape[1], dtype=jnp.int32)
    one_hot = scale_index[:, :, None] == codes[None, None, :]
    if ctx_count == 4 and lax.axis_size("head") % 4 == 0:
        expanded = jnp.repeat(
            jnp.sum(
                jnp.where(one_hot[None], scale_table[:, None, None, :], 0.0), axis=3
            ),
            slot_count // scale_index.shape[1],
            axis=2,
        )
        meta = jnp.concatenate(
            [
                expanded[0] * (inverse * LOG2E),
                expanded[1],
                jnp.broadcast_to(hist_lengths.astype(jnp.float32)[:, None], (8, slot_count)),
            ],
            axis=0,
        )
        flat = gather_and_attend(
            jnp.transpose(queries, (1, 0, 2)),
            cache_keys,
            cache_values,
            meta,
            span_offsets,
            head_groups,
            jnp.transpose(new_keys, (1, 0, 2)),
            jnp.transpose(new_values, (1, 0, 2)),
        )
        return project_and_reduce(flat, out_weight)
    one_hot = one_hot.astype(jnp.float32)
    block_scales = jnp.einsum("kbn,tn->tkb", one_hot, scale_table, precision=lax.Precision.HIGHEST)
    slot_scales = jnp.repeat(block_scales, slot_count // scale_index.shape[1], axis=2)
    head_scales = jnp.take(slot_scales, head_groups, axis=1)
    per_block_key_scales = head_scales[0] * inverse
    value_scales = head_scales[1]
    keys_here = jnp.take(cache_keys, head_groups, axis=0)
    values_here = jnp.take(cache_values, head_groups, axis=0)
    start_slot = entering(hist_lengths, "ctx", add_counts, jnp.zeros_like(hist_lengths))
    slot_ids = jnp.arange(slot_count, dtype=jnp.int32)
    live = slot_ids < hist_lengths[0]
    positions = start_slot[0] + slot_ids

    def block_partial(query_block, source):
        offsets = lax.dynamic_slice_in_dim(span_offsets, source * spans_here, spans_here)
        limits = jnp.repeat(offsets, SPAN)
        visible = live[None, :] & (positions[None, :] < limits[:, None])
        unscaled_scores = jnp.einsum(
            "rhd,hsd->hrs", query_block, keys_here, preferred_element_type=jnp.float32
        )
        logit_scores = unscaled_scores * per_block_key_scales[:, None, :]
        masked = jnp.where(visible[None], logit_scores, floor_score)
        block_top = jnp.max(masked, axis=2)
        block_expo = jnp.where(visible[None], jnp.exp(masked - block_top[:, :, None]), 0.0)
        any_visible = jnp.any(visible, axis=1)
        block_total = jnp.where(any_visible[None, :], jnp.sum(block_expo, axis=2), 1.0)
        weights = (block_expo * value_scales[:, None, :]).astype(jnp.bfloat16)
        mixed = jnp.einsum("hrs,hsd->rhd", weights, values_here, preferred_element_type=jnp.float32)
        mixed = mixed / jnp.transpose(block_total)[:, :, None]
        block_lse = jnp.where(any_visible[None, :], block_top + jnp.log(block_total), floor_score)
        return (mixed.astype(jnp.bfloat16), block_lse)

    def record(parts, lses, source, query_block):
        part, block_lse = block_partial(query_block, source)
        parts = lax.dynamic_update_index_in_dim(parts, part, source, 0)
        lses = lax.dynamic_update_index_in_dim(lses, block_lse, source, 0)
        return (parts, lses)

    def forward(query_block):
        return passed_along(query_block, "ctx", 1)

    parts = jnp.zeros((ctx_count, row_count, heads_here, head_width), jnp.bfloat16)
    lses = jnp.full((ctx_count, heads_here, row_count), floor_score, jnp.float32)
    parts, lses = record(parts, lses, position_me, queries)

    def one_turn(turn, carry):
        travelling, parts_now, lses_now = carry
        travelling = forward(travelling)
        parts_now, lses_now = record(
            parts_now, lses_now, (position_me - turn) % ctx_count, travelling
        )
        return (travelling, parts_now, lses_now)

    travelling, parts, lses = lax.fori_loop(1, ctx_count, one_turn, (queries, parts, lses))
    query_spans = queries.reshape(spans_here, SPAN, heads_here, head_width)
    fresh_keys = jnp.take(new_keys, head_groups, axis=1).reshape(
        spans_here, SPAN, heads_here, head_width
    )
    fresh_values = jnp.take(new_values, head_groups, axis=1).reshape(
        spans_here, SPAN, heads_here, head_width
    )
    causal = jnp.arange(SPAN)[:, None] >= jnp.arange(SPAN)[None, :]
    fresh_raw = (
        jnp.einsum("crhd,cshd->chrs", query_spans, fresh_keys, preferred_element_type=jnp.float32)
        * inverse
    )
    fresh_masked = jnp.where(causal[None, None], fresh_raw, floor_score)
    fresh_top = jnp.max(fresh_masked, axis=3)
    fresh_expo = jnp.where(causal[None, None], jnp.exp(fresh_masked - fresh_top[..., None]), 0.0)
    fresh_total = jnp.sum(fresh_expo, axis=3)
    fresh_weights = fresh_expo.astype(jnp.bfloat16)
    fresh = jnp.einsum(
        "chrs,cshd->crhd", fresh_weights, fresh_values, preferred_element_type=jnp.float32
    )
    fresh = fresh / jnp.transpose(fresh_total, (0, 2, 1))[..., None]
    fresh = fresh.reshape(row_count, heads_here, head_width)
    fresh_lse = jnp.transpose(fresh_top + jnp.log(fresh_total), (1, 0, 2)).reshape(
        heads_here, row_count
    )
    home_parts, home_lses = (
        lax.all_to_all(parts.astype(jnp.float32), "ctx", split_axis=0, concat_axis=0, tiled=True),
        lax.all_to_all(lses, "ctx", split_axis=0, concat_axis=0, tiled=True),
    )
    peak = jnp.maximum(jnp.max(home_lses, axis=0), fresh_lse)
    block_weight = jnp.exp(home_lses - peak[None])
    fresh_weight = jnp.exp(fresh_lse - peak)
    numer_all = jnp.transpose(fresh_weight)[:, :, None] * fresh
    numer_all = numer_all + jnp.sum(
        jnp.transpose(block_weight, (0, 2, 1))[..., None] * home_parts, axis=0
    )
    denom_all = fresh_weight + jnp.sum(block_weight, axis=0)
    attended = (numer_all / jnp.transpose(denom_all)[:, :, None]).astype(jnp.bfloat16)
    flat = attended.reshape(row_count, heads_here * head_width)
    return project_and_reduce(flat, out_weight)


def solution(mesh):
    placed = (
        P("ctx", "head", None),
        P(None, "ctx", None),
        P(None, "ctx", None),
        P(None, "ctx"),
        P(),
        P("ctx"),
        P(),
        P("ctx", None, None),
        P("ctx", None, None),
        P("head"),
        P("head", None),
    )
    return jax.shard_map(
        shards, mesh=mesh, in_specs=placed, out_specs=P("ctx", "head"), check_vma=False
    )
```

```python
import math

import jax
import jax.numpy as jnp
from jax import lax
from jax.experimental import pallas as pl
from jax.experimental.pallas import tpu as pltpu
from jax.sharding import PartitionSpec as P

MESH = pl.DeviceIdType.MESH
LOG2E = math.log2(math.e)

SPAN = 128


floor_score = -1e30


def entering(part, axis, combine, identity):
    place = lax.axis_index(axis)
    gathered = lax.all_gather(part, axis)
    state = jnp.zeros_like(part) + jnp.asarray(identity, part.dtype)

    def one(hop, state):
        return combine(state, lax.dynamic_index_in_dim(gathered, hop, 0, False))

    return lax.fori_loop(0, place, one, state)


def passed_along(value, axis, steps):
    count = lax.axis_size(axis)
    pairs = [(source, (source + steps) % count) for source in range(count)]
    return lax.ppermute(value, axis, pairs)


def add_counts(earlier, later):
    return earlier + later


def project_and_reduce(flat, out_weight):
    heads = lax.axis_size("head")
    planes = heads // 2
    rows, depth = flat.shape
    width = out_weight.shape[1] // heads
    pieces = 4
    piece = rows // pieces
    tile = 256
    slots = 4
    order = [
        sorted(range(planes), key=lambda d, z=z: (-abs(d - z), -d if z < planes // 2 else d))
        for z in range(planes)
    ]

    def kernel(
        flat_ref, weight_ref, out_ref, weights, own, pair_out, pair_in,
        up_out, up_in, down_out, down_in,
        weight_sem, pair_send, pair_recv, up_send, up_recv, down_send, down_recv,
    ):
        me = lax.axis_index("head")
        plane = me // 2
        core = me % 2
        sibling = {"head": 2 * plane + 1 - core}
        above = {"head": me + 2}
        below = {"head": me - 2}
        has_above = plane < planes - 1
        has_below = plane > 0

        def target(step):
            d = jnp.int32(order[0][step])
            for z in range(1, planes):
                d = jnp.where(plane == z, order[z][step], d)
            return d

        targets = [target(step) for step in range(planes)]
        blocks = []
        for d in targets:
            blocks += [2 * d + 1 - core, 2 * d + core]

        def fetch(i):
            column = pl.multiple_of(blocks[i] * width, width)
            return pltpu.make_async_copy(
                weight_ref.at[:, pl.ds(column, width)], weights.at[i % slots], weight_sem.at[i % slots]
            )

        for i in range(slots - 1):
            fetch(i).start()

        barrier = pltpu.get_barrier_semaphore()
        pl.semaphore_signal(barrier, inc=1, device_id=sibling, device_id_type=MESH)

        @pl.when(has_above)
        def _():
            pl.semaphore_signal(barrier, inc=1, device_id=above, device_id_type=MESH)

        @pl.when(has_below)
        def _():
            pl.semaphore_signal(barrier, inc=1, device_id=below, device_id_type=MESH)

        pl.semaphore_wait(barrier, 1 + has_above.astype(jnp.int32) + has_below.astype(jnp.int32))

        def to_sibling(d):
            return pltpu.make_async_remote_copy(
                src_ref=pair_out.at[d], dst_ref=pair_in.at[d],
                send_sem=pair_send.at[d], recv_sem=pair_recv.at[d],
                device_id=sibling, device_id_type=MESH,
            )

        def upward(d, p):
            return pltpu.make_async_remote_copy(
                src_ref=up_out.at[d, p], dst_ref=up_in.at[d, p],
                send_sem=up_send.at[d, p], recv_sem=up_recv.at[d, p],
                device_id=above, device_id_type=MESH,
            )

        def downward(d, p):
            return pltpu.make_async_remote_copy(
                src_ref=down_out.at[d, p], dst_ref=down_in.at[d, p],
                send_sem=down_send.at[d, p], recv_sem=down_recv.at[d, p],
                device_id=below, device_id_type=MESH,
            )

        def multiply(i, store):
            if i + slots - 1 < len(blocks):
                fetch(i + slots - 1).start()
            fetch(i).wait()

            @pl.loop(0, width // tile)
            def _(t):
                columns = pl.ds(pl.multiple_of(t * tile, tile), tile)
                store(
                    columns,
                    jnp.dot(
                        flat_ref[...], weights[i % slots, :, columns],
                        preferred_element_type=jnp.float32,
                    ),
                )

        def combine(d):
            to_sibling(d).wait_recv()

            @pl.loop(0, pieces)
            def _(p):
                span = pl.ds(pl.multiple_of(p * piece, piece), piece)

                @pl.when(d > plane)
                def _():
                    total = own[d, span] + pair_in[d, span].astype(jnp.float32)

                    @pl.when(has_below)
                    def _():
                        upward(d, p).wait_recv()
                        up_out[d, p] = (total + up_in[d, p].astype(jnp.float32)).astype(jnp.bfloat16)

                    @pl.when(jnp.logical_not(has_below))
                    def _():
                        up_out[d, p] = total.astype(jnp.bfloat16)

                    upward(d, p).start()

                @pl.when(d < plane)
                def _():
                    total = own[d, span] + pair_in[d, span].astype(jnp.float32)

                    @pl.when(has_above)
                    def _():
                        downward(d, p).wait_recv()
                        down_out[d, p] = (total + down_in[d, p].astype(jnp.float32)).astype(
                            jnp.bfloat16
                        )

                    @pl.when(jnp.logical_not(has_above))
                    def _():
                        down_out[d, p] = total.astype(jnp.bfloat16)

                    downward(d, p).start()

                @pl.when(d == plane)
                def _():
                    own[d, span] = own[d, span] + pair_in[d, span].astype(jnp.float32)

                    @pl.when(has_below)
                    def _():
                        upward(d, p).wait_recv()
                        own[d, span] = own[d, span] + up_in[d, p].astype(jnp.float32)

                    @pl.when(has_above)
                    def _():
                        downward(d, p).wait_recv()
                        own[d, span] = own[d, span] + down_in[d, p].astype(jnp.float32)

                    out_ref[span] = own[d, span].astype(jnp.bfloat16)

        for step in range(planes):
            d = targets[step]

            def to_pair(columns, value, d=d):
                pair_out[d, :, columns] = value.astype(jnp.bfloat16)

            def to_own(columns, value, d=d):
                own[d, :, columns] = value

            multiply(2 * step, to_pair)
            to_sibling(d).start()
            multiply(2 * step + 1, to_own)
            combine(d)

        for step in range(planes):
            d = targets[step]
            to_sibling(d).wait_send()

            @pl.loop(0, pieces)
            def _(p, d=d):
                @pl.when(d > plane)
                def _():
                    upward(d, p).wait_send()

                @pl.when(d < plane)
                def _():
                    downward(d, p).wait_send()

    block = (planes, rows, width)
    cut = (planes, pieces, piece, width)
    dma = pltpu.SemaphoreType.DMA
    return pl.pallas_call(
        kernel,
        out_shape=jax.ShapeDtypeStruct((rows, width), jnp.bfloat16),
        in_specs=[pl.BlockSpec(memory_space=pltpu.VMEM), pl.BlockSpec(memory_space=pl.ANY)],
        out_specs=pl.BlockSpec(memory_space=pltpu.VMEM),
        scratch_shapes=[
            pltpu.VMEM((slots, depth, width), jnp.bfloat16),
            pltpu.VMEM(block, jnp.float32),
            pltpu.VMEM(block, jnp.bfloat16),
            pltpu.VMEM(block, jnp.bfloat16),
            pltpu.VMEM(cut, jnp.bfloat16),
            pltpu.VMEM(cut, jnp.bfloat16),
            pltpu.VMEM(cut, jnp.bfloat16),
            pltpu.VMEM(cut, jnp.bfloat16),
            dma((slots,)),
            dma((planes,)),
            dma((planes,)),
            dma((planes, pieces)),
            dma((planes, pieces)),
            dma((planes, pieces)),
            dma((planes, pieces)),
        ],
        compiler_params=pltpu.CompilerParams(
            collective_id=1, has_side_effects=True, vmem_limit_bytes=56 * 1024 * 1024
        ),
        cost_estimate=pl.CostEstimate(
            flops=2 * rows * depth * width * heads,
            bytes_accessed=2 * depth * width * heads,
            transcendentals=0,
        ),
        name="project_and_reduce",
    )(flat, out_weight)


def gather_and_attend(queries, keys, values, meta, offsets, groups, fresh_keys, fresh_values):
    heads_here, row_count, head_width = queries.shape
    group_count, slot_count, _ = keys.shape
    half = slot_count // 2
    near = group_count // 2
    spans_here = row_count // SPAN
    factor = LOG2E / math.sqrt(head_width)

    def kernel(
        offsets_ref, groups_ref, q_ref, k_ref, v_ref, meta_ref, fk_ref, fv_ref, out_ref,
        xf_k, xf_v, xs_k, xs_v, yf_k, yf_v, ys_k, ys_v, dn_k, dn_v, df_k, df_v,
        meta_x, meta_y, meta_d, bias, top, total, mixed,
        send, recv, meta_send, meta_recv,
    ):
        me = lax.axis_index("ctx")
        head = lax.axis_index("head")
        plane = head // 2
        core = head % 2
        parity = plane % 2
        x_place = me + 1 - 2 * (me % 2)
        y_place = (me + 2) % 4
        d_place = 3 - me
        to_x, to_y, to_d = {"ctx": x_place}, {"ctx": y_place}, {"ctx": d_place}
        sibling = {"head": 2 * plane + 1 - core}
        partner = {"head": head + 2 - 4 * parity}
        barrier = pltpu.get_barrier_semaphore()
        for device in (to_x, to_y, to_d, sibling, partner):
            pl.semaphore_signal(barrier, inc=1, device_id=device, device_id_type=MESH)
        pl.semaphore_wait(barrier, 5)

        mine = pl.ds(core * near, near)
        low = pl.ds(core * near, near // 2)
        high = pl.ds(core * near + near // 2, near // 2)
        first = pl.multiple_of(parity * half, 128)
        second = pl.multiple_of((1 - parity) * half, 128)
        started = []

        def copy(source, target, device):
            i = len(started)
            made = pltpu.make_async_remote_copy(
                src_ref=source, dst_ref=target, send_sem=send.at[i], recv_sem=recv.at[i],
                device_id=device, device_id_type=MESH,
            )
            made.start()
            started.append(made)
            return made

        meta_copies = []
        for i, (target, device) in enumerate(((meta_x, to_x), (meta_y, to_y), (meta_d, to_d))):
            made = pltpu.make_async_remote_copy(
                src_ref=meta_ref, dst_ref=target, send_sem=meta_send.at[i], recv_sem=meta_recv.at[i],
                device_id=device, device_id_type=MESH,
            )
            made.start()
            meta_copies.append(made)

        def own(ref, offset):
            slots = pl.ds(offset, half)
            return ref.at[mine, slots] if ref is k_ref else ref.at[mine, :, slots]

        firsts = [
            copy(own(ref, first), target.at[mine], device)
            for ref, tx, ty in ((k_ref, xf_k, yf_k), (v_ref, xf_v, yf_v))
            for target, device in ((tx, to_x), (ty, to_y))
        ]

        def fresh_head(h, carry):
            g = groups_ref[h]
            for t in range(spans_here):
                span = pl.ds(t * SPAN, SPAN)
                scores = lax.dot_general(
                    fk_ref[g, span], q_ref[h, span], (((1,), (1,)), ((), ())),
                    preferred_element_type=jnp.float32,
                ) * factor
                causal = lax.broadcasted_iota(jnp.int32, scores.shape, 1) >= lax.broadcasted_iota(
                    jnp.int32, scores.shape, 0
                )
                scores = jnp.where(causal, scores, floor_score)
                largest = jnp.max(scores, axis=0, keepdims=True)
                expo = jnp.exp2(scores - largest)
                top[h, :, span] = largest
                total[h, :, span] = jnp.sum(expo, axis=0, keepdims=True)
                mixed[h, :, span] = jnp.dot(
                    fv_ref[g, :, span], expo.astype(jnp.bfloat16),
                    preferred_element_type=jnp.float32,
                )
            return carry

        lax.fori_loop(0, heads_here, fresh_head, 0, unroll=2)
        for made in meta_copies:
            made.wait_recv()

        places = ((me, meta_ref), (x_place, meta_x), (y_place, meta_y), (d_place, meta_d))
        slot_ids = lax.broadcasted_iota(jnp.int32, (slot_count, SPAN), 0)
        lengths = [
            m[2 * group_count, :, pl.ds(0, SPAN)].astype(jnp.int32) for _, m in places
        ]
        for b, (place, _) in enumerate(places):
            start = jnp.zeros((1, SPAN), jnp.int32)
            for (other, _), length in zip(places, lengths):
                start = start + jnp.where(other < place, length, 0)
            for t in range(spans_here):
                limit = jnp.minimum(lengths[b], offsets_ref[me * spans_here + t] - start)
                bias[b, :, pl.ds(t * SPAN, SPAN)] = jnp.where(slot_ids < limit, 0.0, floor_score)

        def attend(b, offset, size, keys_of, values_of):
            meta_of = places[b][1]

            def scales(row, j):
                part = meta_of[row, :, pl.ds(offset + j * SPAN, SPAN)]
                return jnp.concatenate([part] * spans_here, axis=1)

            def one(h, carry):
                g = groups_ref[h]
                raw = lax.dot_general(
                    keys_of(g), q_ref[h], (((1,), (1,)), ((), ())),
                    preferred_element_type=jnp.float32,
                )
                scores = [
                    raw[j * SPAN:(j + 1) * SPAN] * scales(g, j)
                    + bias[b, pl.ds(offset + j * SPAN, SPAN), :]
                    for j in range(size // SPAN)
                ]
                before = top[h]
                largest = before
                for score in scores:
                    largest = jnp.maximum(largest, jnp.max(score, axis=0, keepdims=True))
                keep = jnp.exp2(before - largest)
                added = total[h] * keep
                weights = []
                for j, score in enumerate(scores):
                    expo = jnp.exp2(score - largest)
                    added = added + jnp.sum(expo, axis=0, keepdims=True)
                    weights.append((expo * scales(g + group_count, j)).astype(jnp.bfloat16))
                top[h] = largest
                total[h] = added
                mixed[h] = mixed[h] * keep + jnp.dot(
                    values_of(g), jnp.concatenate(weights, axis=0),
                    preferred_element_type=jnp.float32,
                )
                return carry

            lax.fori_loop(0, heads_here, one, 0, unroll=2)

        def attend_ref(b, offset, k, v):
            attend(b, offset, half, lambda g: k[g], lambda g: v[g])

        attend(0, 0, slot_count, lambda g: k_ref[g], lambda g: v_ref[g])

        def share(pairs):
            return [copy(ref.at[part], ref.at[part], sibling) for ref, part in pairs]

        def arrived(copies):
            for made in copies:
                made.wait_recv()

        arrived(firsts)
        relays = [
            copy(source.at[part], target.at[part], device)
            for source, target, part, device in (
                (xf_k, dn_k, low, to_y), (yf_k, dn_k, high, to_x),
                (xf_v, dn_v, low, to_y), (yf_v, dn_v, high, to_x),
            )
        ]
        seconds = [
            copy(own(ref, second), target.at[mine], device)
            for ref, tx, ty in ((k_ref, xs_k, ys_k), (v_ref, xs_v, ys_v))
            for target, device in ((tx, to_x), (ty, to_y))
        ]
        arrived(share([(xf_k, mine), (xf_v, mine), (yf_k, mine), (yf_v, mine)]))
        attend_ref(1, first, xf_k, xf_v)
        arrived(relays)
        across = [
            copy(source.at[part], target.at[part], partner)
            for source, target in ((dn_k, df_k), (dn_v, df_v))
            for part in (low, high)
        ]
        near_shared = share([(dn_k, mine), (dn_v, mine)])
        attend_ref(2, first, yf_k, yf_v)
        arrived(near_shared)
        attend_ref(3, first, dn_k, dn_v)
        arrived(seconds)
        second_shared = share([(xs_k, mine), (xs_v, mine), (ys_k, mine), (ys_v, mine)])
        arrived(across)
        far_shared = share([(df_k, mine), (df_v, mine)])
        arrived(second_shared)
        attend_ref(1, second, xs_k, xs_v)
        attend_ref(2, second, ys_k, ys_v)
        arrived(far_shared)
        attend_ref(3, second, df_k, df_v)

        def finish(h, carry):
            columns = pl.ds(pl.multiple_of(h * head_width, head_width), head_width)
            out_ref[:, columns] = jnp.transpose(mixed[h] / total[h]).astype(jnp.bfloat16)
            return carry

        lax.fori_loop(0, heads_here, finish, 0)
        for made in started + meta_copies:
            made.wait_send()

    key_chunk = pltpu.VMEM((group_count, half, head_width), jnp.bfloat16)
    value_chunk = pltpu.VMEM((group_count, head_width, half), jnp.bfloat16)
    table = pltpu.VMEM(meta.shape, jnp.float32)
    dma = pltpu.SemaphoreType.DMA
    copies = 4 + 4 + 4 + 4 + 4 + 2 + 4 + 2
    whole = pl.BlockSpec(memory_space=pltpu.VMEM)
    scalar = pl.BlockSpec(memory_space=pltpu.SMEM)
    return pl.pallas_call(
        kernel,
        out_shape=jax.ShapeDtypeStruct((row_count, heads_here * head_width), jnp.bfloat16),
        in_specs=[scalar, scalar] + [whole] * 6,
        out_specs=whole,
        scratch_shapes=[key_chunk, value_chunk] * 6
        + [table] * 3
        + [
            pltpu.VMEM((4, slot_count, row_count), jnp.float32),
            pltpu.VMEM((heads_here, 1, row_count), jnp.float32),
            pltpu.VMEM((heads_here, 1, row_count), jnp.float32),
            pltpu.VMEM((heads_here, head_width, row_count), jnp.float32),
            dma((copies,)),
            dma((copies,)),
            dma((3,)),
            dma((3,)),
        ],
        compiler_params=pltpu.CompilerParams(
            collective_id=2, has_side_effects=True, vmem_limit_bytes=56 * 1024 * 1024
        ),
        cost_estimate=pl.CostEstimate(
            flops=16 * row_count * heads_here * slot_count * head_width,
            bytes_accessed=8 * group_count * slot_count * head_width,
            transcendentals=4 * row_count * heads_here * slot_count,
        ),
        name="gather_and_attend",
    )(offsets, groups, queries, keys, values, meta, fresh_keys, fresh_values)


def shards(
    queries,
    cache_keys,
    cache_values,
    scale_index,
    scale_table,
    hist_lengths,
    span_offsets,
    new_keys,
    new_values,
    head_groups,
    out_weight,
):
    ctx_count = lax.axis_size("ctx")
    position_me = lax.axis_index("ctx")
    row_count, heads_here, head_width = queries.shape
    slot_count = cache_keys.shape[1]
    spans_here = row_count // SPAN
    inverse = 1.0 / math.sqrt(head_width)
    codes = jnp.arange(scale_table.shape[1], dtype=jnp.int32)
    one_hot = scale_index[:, :, None] == codes[None, None, :]
    if ctx_count == 4 and lax.axis_size("head") % 4 == 0:
        expanded = jnp.repeat(
            jnp.sum(
                jnp.where(one_hot[None], scale_table[:, None, None, :], 0.0), axis=3
            ),
            slot_count // scale_index.shape[1],
            axis=2,
        )
        meta = jnp.concatenate(
            [
                expanded[0] * (inverse * LOG2E),
                expanded[1],
                jnp.broadcast_to(hist_lengths.astype(jnp.float32)[:, None], (8, slot_count)),
            ],
            axis=0,
        )
        flat = gather_and_attend(
            jnp.transpose(queries, (1, 0, 2)),
            cache_keys,
            jnp.transpose(cache_values, (0, 2, 1)),
            meta[:, None, :],
            span_offsets,
            head_groups,
            jnp.transpose(new_keys, (1, 0, 2)),
            jnp.transpose(new_values, (1, 2, 0)),
        )
        return project_and_reduce(flat, out_weight)
    one_hot = one_hot.astype(jnp.float32)
    block_scales = jnp.einsum("kbn,tn->tkb", one_hot, scale_table, precision=lax.Precision.HIGHEST)
    slot_scales = jnp.repeat(block_scales, slot_count // scale_index.shape[1], axis=2)
    head_scales = jnp.take(slot_scales, head_groups, axis=1)
    per_block_key_scales = head_scales[0] * inverse
    value_scales = head_scales[1]
    keys_here = jnp.take(cache_keys, head_groups, axis=0)
    values_here = jnp.take(cache_values, head_groups, axis=0)
    start_slot = entering(hist_lengths, "ctx", add_counts, jnp.zeros_like(hist_lengths))
    slot_ids = jnp.arange(slot_count, dtype=jnp.int32)
    live = slot_ids < hist_lengths[0]
    positions = start_slot[0] + slot_ids

    def block_partial(query_block, source):
        offsets = lax.dynamic_slice_in_dim(span_offsets, source * spans_here, spans_here)
        limits = jnp.repeat(offsets, SPAN)
        visible = live[None, :] & (positions[None, :] < limits[:, None])
        unscaled_scores = jnp.einsum(
            "rhd,hsd->hrs", query_block, keys_here, preferred_element_type=jnp.float32
        )
        logit_scores = unscaled_scores * per_block_key_scales[:, None, :]
        masked = jnp.where(visible[None], logit_scores, floor_score)
        block_top = jnp.max(masked, axis=2)
        block_expo = jnp.where(visible[None], jnp.exp(masked - block_top[:, :, None]), 0.0)
        any_visible = jnp.any(visible, axis=1)
        block_total = jnp.where(any_visible[None, :], jnp.sum(block_expo, axis=2), 1.0)
        weights = (block_expo * value_scales[:, None, :]).astype(jnp.bfloat16)
        mixed = jnp.einsum("hrs,hsd->rhd", weights, values_here, preferred_element_type=jnp.float32)
        mixed = mixed / jnp.transpose(block_total)[:, :, None]
        block_lse = jnp.where(any_visible[None, :], block_top + jnp.log(block_total), floor_score)
        return (mixed.astype(jnp.bfloat16), block_lse)

    def record(parts, lses, source, query_block):
        part, block_lse = block_partial(query_block, source)
        parts = lax.dynamic_update_index_in_dim(parts, part, source, 0)
        lses = lax.dynamic_update_index_in_dim(lses, block_lse, source, 0)
        return (parts, lses)

    def forward(query_block):
        return passed_along(query_block, "ctx", 1)

    parts = jnp.zeros((ctx_count, row_count, heads_here, head_width), jnp.bfloat16)
    lses = jnp.full((ctx_count, heads_here, row_count), floor_score, jnp.float32)
    parts, lses = record(parts, lses, position_me, queries)

    def one_turn(turn, carry):
        travelling, parts_now, lses_now = carry
        travelling = forward(travelling)
        parts_now, lses_now = record(
            parts_now, lses_now, (position_me - turn) % ctx_count, travelling
        )
        return (travelling, parts_now, lses_now)

    travelling, parts, lses = lax.fori_loop(1, ctx_count, one_turn, (queries, parts, lses))
    query_spans = queries.reshape(spans_here, SPAN, heads_here, head_width)
    fresh_keys = jnp.take(new_keys, head_groups, axis=1).reshape(
        spans_here, SPAN, heads_here, head_width
    )
    fresh_values = jnp.take(new_values, head_groups, axis=1).reshape(
        spans_here, SPAN, heads_here, head_width
    )
    causal = jnp.arange(SPAN)[:, None] >= jnp.arange(SPAN)[None, :]
    fresh_raw = (
        jnp.einsum("crhd,cshd->chrs", query_spans, fresh_keys, preferred_element_type=jnp.float32)
        * inverse
    )
    fresh_masked = jnp.where(causal[None, None], fresh_raw, floor_score)
    fresh_top = jnp.max(fresh_masked, axis=3)
    fresh_expo = jnp.where(causal[None, None], jnp.exp(fresh_masked - fresh_top[..., None]), 0.0)
    fresh_total = jnp.sum(fresh_expo, axis=3)
    fresh_weights = fresh_expo.astype(jnp.bfloat16)
    fresh = jnp.einsum(
        "chrs,cshd->crhd", fresh_weights, fresh_values, preferred_element_type=jnp.float32
    )
    fresh = fresh / jnp.transpose(fresh_total, (0, 2, 1))[..., None]
    fresh = fresh.reshape(row_count, heads_here, head_width)
    fresh_lse = jnp.transpose(fresh_top + jnp.log(fresh_total), (1, 0, 2)).reshape(
        heads_here, row_count
    )
    home_parts, home_lses = (
        lax.all_to_all(parts.astype(jnp.float32), "ctx", split_axis=0, concat_axis=0, tiled=True),
        lax.all_to_all(lses, "ctx", split_axis=0, concat_axis=0, tiled=True),
    )
    peak = jnp.maximum(jnp.max(home_lses, axis=0), fresh_lse)
    block_weight = jnp.exp(home_lses - peak[None])
    fresh_weight = jnp.exp(fresh_lse - peak)
    numer_all = jnp.transpose(fresh_weight)[:, :, None] * fresh
    numer_all = numer_all + jnp.sum(
        jnp.transpose(block_weight, (0, 2, 1))[..., None] * home_parts, axis=0
    )
    denom_all = fresh_weight + jnp.sum(block_weight, axis=0)
    attended = (numer_all / jnp.transpose(denom_all)[:, :, None]).astype(jnp.bfloat16)
    flat = attended.reshape(row_count, heads_here * head_width)
    return project_and_reduce(flat, out_weight)


def solution(mesh):
    placed = (
        P("ctx", "head", None),
        P(None, "ctx", None),
        P(None, "ctx", None),
        P(None, "ctx"),
        P(),
        P("ctx"),
        P(),
        P("ctx", None, None),
        P("ctx", None, None),
        P("head"),
        P("head", None),
    )
    return jax.shard_map(
        shards, mesh=mesh, in_specs=placed, out_specs=P("ctx", "head"), check_vma=False
    )
```

```python
import math

import jax
import jax.numpy as jnp
from jax import lax
from jax.experimental import pallas as pl
from jax.experimental.pallas import tpu as pltpu
from jax.sharding import PartitionSpec as P

MESH = pl.DeviceIdType.MESH
LOG2E = math.log2(math.e)

SPAN = 128


floor_score = -1e30


def entering(part, axis, combine, identity):
    place = lax.axis_index(axis)
    gathered = lax.all_gather(part, axis)
    state = jnp.zeros_like(part) + jnp.asarray(identity, part.dtype)

    def one(hop, state):
        return combine(state, lax.dynamic_index_in_dim(gathered, hop, 0, False))

    return lax.fori_loop(0, place, one, state)


def passed_along(value, axis, steps):
    count = lax.axis_size(axis)
    pairs = [(source, (source + steps) % count) for source in range(count)]
    return lax.ppermute(value, axis, pairs)


def add_counts(earlier, later):
    return earlier + later


def project_and_reduce(flat, out_weight):
    heads = lax.axis_size("head")
    planes = heads // 2
    rows, depth = flat.shape
    width = out_weight.shape[1] // heads
    pieces = 8
    flying = 4
    piece = rows // pieces
    tile = 256
    slots = 4
    order = [
        sorted(range(planes), key=lambda d, z=z: (-abs(d - z), d if z < planes // 2 else -d))
        for z in range(planes)
    ]

    def kernel(
        flat_ref, weight_ref, out_ref, weights, own, pair_out, pair_in,
        up_out, up_in, down_out, down_in,
        weight_sem, pair_send, pair_recv, up_send, up_recv, down_send, down_recv,
    ):
        me = lax.axis_index("head")
        plane = me // 2
        core = me % 2
        sibling = {"head": 2 * plane + 1 - core}
        above = {"head": me + 2}
        below = {"head": me - 2}
        has_above = plane < planes - 1
        has_below = plane > 0

        def target(step):
            d = jnp.int32(order[0][step])
            for z in range(1, planes):
                d = jnp.where(plane == z, order[z][step], d)
            return d

        targets = [target(step) for step in range(planes)]
        blocks = []
        for d in targets:
            blocks += [2 * d + 1 - core, 2 * d + core]

        def fetch(i):
            column = pl.multiple_of(blocks[i] * width, width)
            return pltpu.make_async_copy(
                weight_ref.at[:, pl.ds(column, width)], weights.at[i % slots], weight_sem.at[i % slots]
            )

        for i in range(slots - 1):
            fetch(i).start()

        barrier = pltpu.get_barrier_semaphore()
        pl.semaphore_signal(barrier, inc=1, device_id=sibling, device_id_type=MESH)

        @pl.when(has_above)
        def _():
            pl.semaphore_signal(barrier, inc=1, device_id=above, device_id_type=MESH)

        @pl.when(has_below)
        def _():
            pl.semaphore_signal(barrier, inc=1, device_id=below, device_id_type=MESH)

        pl.semaphore_wait(barrier, 1 + has_above.astype(jnp.int32) + has_below.astype(jnp.int32))

        def to_sibling(d):
            return pltpu.make_async_remote_copy(
                src_ref=pair_out.at[d], dst_ref=pair_in.at[d],
                send_sem=pair_send.at[d], recv_sem=pair_recv.at[d],
                device_id=sibling, device_id_type=MESH,
            )

        def upward(d, p):
            return pltpu.make_async_remote_copy(
                src_ref=up_out.at[d, p], dst_ref=up_in.at[d, p],
                send_sem=up_send.at[d, p], recv_sem=up_recv.at[d, p],
                device_id=above, device_id_type=MESH,
            )

        def downward(d, p):
            return pltpu.make_async_remote_copy(
                src_ref=down_out.at[d, p], dst_ref=down_in.at[d, p],
                send_sem=down_send.at[d, p], recv_sem=down_recv.at[d, p],
                device_id=below, device_id_type=MESH,
            )

        def multiply(i, store):
            if i + slots - 1 < len(blocks):
                fetch(i + slots - 1).start()
            fetch(i).wait()

            @pl.loop(0, width // tile)
            def _(t):
                columns = pl.ds(pl.multiple_of(t * tile, tile), tile)
                store(
                    columns,
                    jnp.dot(
                        flat_ref[...], weights[i % slots, :, columns],
                        preferred_element_type=jnp.float32,
                    ),
                )

        def combine(d):
            to_sibling(d).wait_recv()

            @pl.loop(0, pieces)
            def _(p):
                span = pl.ds(pl.multiple_of(p * piece, piece), piece)

                @pl.when(d > plane)
                def _():
                    total = own[d, span] + pair_in[d, span].astype(jnp.float32)

                    @pl.when(has_below)
                    def _():
                        upward(d, p).wait_recv()
                        up_out[d, p] = (total + up_in[d, p].astype(jnp.float32)).astype(jnp.bfloat16)

                    @pl.when(jnp.logical_not(has_below))
                    def _():
                        up_out[d, p] = total.astype(jnp.bfloat16)

                    @pl.when(p >= flying)
                    def _():
                        upward(d, p - flying).wait_send()

                    @pl.when((p < flying) & (d < planes - 1))
                    def _():
                        upward(d + 1, p + pieces - flying).wait_send()

                    upward(d, p).start()

                @pl.when(d < plane)
                def _():
                    total = own[d, span] + pair_in[d, span].astype(jnp.float32)

                    @pl.when(has_above)
                    def _():
                        downward(d, p).wait_recv()
                        down_out[d, p] = (total + down_in[d, p].astype(jnp.float32)).astype(
                            jnp.bfloat16
                        )

                    @pl.when(jnp.logical_not(has_above))
                    def _():
                        down_out[d, p] = total.astype(jnp.bfloat16)

                    @pl.when(p >= flying)
                    def _():
                        downward(d, p - flying).wait_send()

                    @pl.when((p < flying) & (d > 0))
                    def _():
                        downward(d - 1, p + pieces - flying).wait_send()

                    downward(d, p).start()

                @pl.when(d == plane)
                def _():
                    own[d, span] = own[d, span] + pair_in[d, span].astype(jnp.float32)

                    @pl.when(has_below)
                    def _():
                        upward(d, p).wait_recv()
                        own[d, span] = own[d, span] + up_in[d, p].astype(jnp.float32)

                    @pl.when(has_above)
                    def _():
                        downward(d, p).wait_recv()
                        own[d, span] = own[d, span] + down_in[d, p].astype(jnp.float32)

                    out_ref[span] = own[d, span].astype(jnp.bfloat16)

        for step in range(planes):
            d = targets[step]

            def to_pair(columns, value, d=d):
                pair_out[d, :, columns] = value.astype(jnp.bfloat16)

            def to_own(columns, value, d=d):
                own[d, :, columns] = value

            multiply(2 * step, to_pair)
            to_sibling(d).start()
            multiply(2 * step + 1, to_own)
            combine(d)

        for d in targets:
            to_sibling(d).wait_send()

        @pl.loop(pieces - flying, pieces)
        def _(p):
            @pl.when(has_above)
            def _():
                upward(plane + 1, p).wait_send()

            @pl.when(has_below)
            def _():
                downward(plane - 1, p).wait_send()

    block = (planes, rows, width)
    cut = (planes, pieces, piece, width)
    dma = pltpu.SemaphoreType.DMA
    return pl.pallas_call(
        kernel,
        out_shape=jax.ShapeDtypeStruct((rows, width), jnp.bfloat16),
        in_specs=[pl.BlockSpec(memory_space=pltpu.VMEM), pl.BlockSpec(memory_space=pl.ANY)],
        out_specs=pl.BlockSpec(memory_space=pltpu.VMEM),
        scratch_shapes=[
            pltpu.VMEM((slots, depth, width), jnp.bfloat16),
            pltpu.VMEM(block, jnp.float32),
            pltpu.VMEM(block, jnp.bfloat16),
            pltpu.VMEM(block, jnp.bfloat16),
            pltpu.VMEM(cut, jnp.bfloat16),
            pltpu.VMEM(cut, jnp.bfloat16),
            pltpu.VMEM(cut, jnp.bfloat16),
            pltpu.VMEM(cut, jnp.bfloat16),
            dma((slots,)),
            dma((planes,)),
            dma((planes,)),
            dma((planes, pieces)),
            dma((planes, pieces)),
            dma((planes, pieces)),
            dma((planes, pieces)),
        ],
        compiler_params=pltpu.CompilerParams(
            collective_id=1, has_side_effects=True, vmem_limit_bytes=56 * 1024 * 1024
        ),
        cost_estimate=pl.CostEstimate(
            flops=2 * rows * depth * width * heads,
            bytes_accessed=2 * depth * width * heads,
            transcendentals=0,
        ),
        name="project_and_reduce",
    )(flat, out_weight)


def gather_and_attend(queries, keys, values, meta, offsets, groups, fresh_keys, fresh_values):
    heads_here, row_count, head_width = queries.shape
    group_count, slot_count, _ = keys.shape
    half = slot_count // 2
    near = group_count // 2
    spans_here = row_count // SPAN
    factor = LOG2E / math.sqrt(head_width)

    def kernel(
        offsets_ref, groups_ref, q_ref, k_ref, v_ref, meta_ref, fk_ref, fv_ref, out_ref,
        xf_k, xf_v, xs_k, xs_v, yf_k, yf_v, ys_k, ys_v, dn_k, dn_v, df_k, df_v,
        meta_x, meta_y, meta_d, bias, top, total, mixed,
        send, recv, meta_send, meta_recv,
    ):
        me = lax.axis_index("ctx")
        head = lax.axis_index("head")
        plane = head // 2
        core = head % 2
        parity = plane % 2
        x_place = me + 1 - 2 * (me % 2)
        y_place = (me + 2) % 4
        d_place = 3 - me
        to_x, to_y, to_d = {"ctx": x_place}, {"ctx": y_place}, {"ctx": d_place}
        sibling = {"head": 2 * plane + 1 - core}
        partner = {"head": head + 2 - 4 * parity}
        barrier = pltpu.get_barrier_semaphore()
        for device in (to_x, to_y, to_d, sibling, partner):
            pl.semaphore_signal(barrier, inc=1, device_id=device, device_id_type=MESH)
        pl.semaphore_wait(barrier, 5)

        mine = pl.ds(core * near, near)
        low = pl.ds(core * near, near // 2)
        high = pl.ds(core * near + near // 2, near // 2)
        first = pl.multiple_of(parity * half, 128)
        second = pl.multiple_of((1 - parity) * half, 128)
        started = []

        def copy(source, target, device):
            i = len(started)
            made = pltpu.make_async_remote_copy(
                src_ref=source, dst_ref=target, send_sem=send.at[i], recv_sem=recv.at[i],
                device_id=device, device_id_type=MESH,
            )
            made.start()
            started.append(made)
            return made

        meta_copies = []
        for i, (target, device) in enumerate(((meta_x, to_x), (meta_y, to_y), (meta_d, to_d))):
            made = pltpu.make_async_remote_copy(
                src_ref=meta_ref, dst_ref=target, send_sem=meta_send.at[i], recv_sem=meta_recv.at[i],
                device_id=device, device_id_type=MESH,
            )
            made.start()
            meta_copies.append(made)

        def own(ref, offset):
            slots = pl.ds(offset, half)
            return ref.at[mine, slots] if ref is k_ref else ref.at[mine, :, slots]

        firsts = [
            copy(own(ref, first), target.at[mine], device)
            for ref, tx, ty in ((k_ref, xf_k, yf_k), (v_ref, xf_v, yf_v))
            for target, device in ((tx, to_x), (ty, to_y))
        ]

        def fresh_head(h, carry):
            g = groups_ref[h]
            for t in range(spans_here):
                span = pl.ds(t * SPAN, SPAN)
                scores = lax.dot_general(
                    fk_ref[g, span], q_ref[h, span], (((1,), (1,)), ((), ())),
                    preferred_element_type=jnp.float32,
                ) * factor
                causal = lax.broadcasted_iota(jnp.int32, scores.shape, 1) >= lax.broadcasted_iota(
                    jnp.int32, scores.shape, 0
                )
                scores = jnp.where(causal, scores, floor_score)
                largest = jnp.max(scores, axis=0, keepdims=True)
                expo = jnp.exp2(scores - largest)
                top[h, :, span] = largest
                total[h, :, span] = jnp.sum(expo, axis=0, keepdims=True)
                mixed[h, :, span] = jnp.dot(
                    fv_ref[g, :, span], expo.astype(jnp.bfloat16),
                    preferred_element_type=jnp.float32,
                )
            return carry

        lax.fori_loop(0, heads_here, fresh_head, 0, unroll=2)
        for made in meta_copies:
            made.wait_recv()

        places = ((me, meta_ref), (x_place, meta_x), (y_place, meta_y), (d_place, meta_d))
        slot_ids = lax.broadcasted_iota(jnp.int32, (slot_count, SPAN), 0)
        lengths = [
            m[2 * group_count, :, pl.ds(0, SPAN)].astype(jnp.int32) for _, m in places
        ]
        for b, (place, _) in enumerate(places):
            start = jnp.zeros((1, SPAN), jnp.int32)
            for (other, _), length in zip(places, lengths):
                start = start + jnp.where(other < place, length, 0)
            for t in range(spans_here):
                limit = jnp.minimum(lengths[b], offsets_ref[me * spans_here + t] - start)
                bias[b, :, pl.ds(t * SPAN, SPAN)] = jnp.where(slot_ids < limit, 0.0, floor_score)

        def attend(b, offset, size, keys_of, values_of):
            meta_of = places[b][1]

            def scales(row, j):
                part = meta_of[row, :, pl.ds(offset + j * SPAN, SPAN)]
                return jnp.concatenate([part] * spans_here, axis=1)

            def one(h, carry):
                g = groups_ref[h]
                raw = lax.dot_general(
                    keys_of(g), q_ref[h], (((1,), (1,)), ((), ())),
                    preferred_element_type=jnp.float32,
                )
                scores = [
                    raw[j * SPAN:(j + 1) * SPAN] * scales(g, j)
                    + bias[b, pl.ds(offset + j * SPAN, SPAN), :]
                    for j in range(size // SPAN)
                ]
                before = top[h]
                largest = before
                for score in scores:
                    largest = jnp.maximum(largest, jnp.max(score, axis=0, keepdims=True))
                keep = jnp.exp2(before - largest)
                added = total[h] * keep
                weights = []
                for j, score in enumerate(scores):
                    expo = jnp.exp2(score - largest)
                    added = added + jnp.sum(expo, axis=0, keepdims=True)
                    weights.append((expo * scales(g + group_count, j)).astype(jnp.bfloat16))
                top[h] = largest
                total[h] = added
                mixed[h] = mixed[h] * keep + jnp.dot(
                    values_of(g), jnp.concatenate(weights, axis=0),
                    preferred_element_type=jnp.float32,
                )
                return carry

            lax.fori_loop(0, heads_here, one, 0, unroll=2)

        def attend_ref(b, offset, k, v):
            attend(b, offset, half, lambda g: k[g], lambda g: v[g])

        attend(0, 0, slot_count, lambda g: k_ref[g], lambda g: v_ref[g])

        def share(pairs):
            return [copy(ref.at[part], ref.at[part], sibling) for ref, part in pairs]

        def arrived(copies):
            for made in copies:
                made.wait_recv()

        arrived(firsts)
        relays = [
            copy(source.at[part], target.at[part], device)
            for source, target, part, device in (
                (xf_k, dn_k, low, to_y), (yf_k, dn_k, high, to_x),
                (xf_v, dn_v, low, to_y), (yf_v, dn_v, high, to_x),
            )
        ]
        arrived(share([(xf_k, mine), (xf_v, mine), (yf_k, mine), (yf_v, mine)]))
        attend_ref(1, first, xf_k, xf_v)
        seconds = [
            copy(own(ref, second), target.at[mine], device)
            for ref, tx, ty in ((k_ref, xs_k, ys_k), (v_ref, xs_v, ys_v))
            for target, device in ((tx, to_x), (ty, to_y))
        ]
        arrived(relays)
        across = [
            copy(source.at[part], target.at[part], partner)
            for source, target in ((dn_k, df_k), (dn_v, df_v))
            for part in (low, high)
        ]
        near_shared = share([(dn_k, mine), (dn_v, mine)])
        attend_ref(2, first, yf_k, yf_v)
        arrived(near_shared)
        attend_ref(3, first, dn_k, dn_v)
        arrived(seconds)
        second_shared = share([(xs_k, mine), (xs_v, mine), (ys_k, mine), (ys_v, mine)])
        arrived(second_shared)
        attend_ref(1, second, xs_k, xs_v)
        arrived(across)
        far_shared = share([(df_k, mine), (df_v, mine)])
        attend_ref(2, second, ys_k, ys_v)
        arrived(far_shared)
        attend_ref(3, second, df_k, df_v)

        def finish(h, carry):
            columns = pl.ds(pl.multiple_of(h * head_width, head_width), head_width)
            out_ref[:, columns] = jnp.transpose(mixed[h] / total[h]).astype(jnp.bfloat16)
            return carry

        lax.fori_loop(0, heads_here, finish, 0)
        for made in started + meta_copies:
            made.wait_send()

    key_chunk = pltpu.VMEM((group_count, half, head_width), jnp.bfloat16)
    value_chunk = pltpu.VMEM((group_count, head_width, half), jnp.bfloat16)
    table = pltpu.VMEM(meta.shape, jnp.float32)
    dma = pltpu.SemaphoreType.DMA
    copies = 4 + 4 + 4 + 4 + 4 + 2 + 4 + 2
    whole = pl.BlockSpec(memory_space=pltpu.VMEM)
    scalar = pl.BlockSpec(memory_space=pltpu.SMEM)
    return pl.pallas_call(
        kernel,
        out_shape=jax.ShapeDtypeStruct((row_count, heads_here * head_width), jnp.bfloat16),
        in_specs=[scalar, scalar] + [whole] * 6,
        out_specs=whole,
        scratch_shapes=[key_chunk, value_chunk] * 6
        + [table] * 3
        + [
            pltpu.VMEM((4, slot_count, row_count), jnp.float32),
            pltpu.VMEM((heads_here, 1, row_count), jnp.float32),
            pltpu.VMEM((heads_here, 1, row_count), jnp.float32),
            pltpu.VMEM((heads_here, head_width, row_count), jnp.float32),
            dma((copies,)),
            dma((copies,)),
            dma((3,)),
            dma((3,)),
        ],
        compiler_params=pltpu.CompilerParams(
            collective_id=2, has_side_effects=True, vmem_limit_bytes=56 * 1024 * 1024
        ),
        cost_estimate=pl.CostEstimate(
            flops=16 * row_count * heads_here * slot_count * head_width,
            bytes_accessed=8 * group_count * slot_count * head_width,
            transcendentals=4 * row_count * heads_here * slot_count,
        ),
        name="gather_and_attend",
    )(offsets, groups, queries, keys, values, meta, fresh_keys, fresh_values)


def shards(
    queries,
    cache_keys,
    cache_values,
    scale_index,
    scale_table,
    hist_lengths,
    span_offsets,
    new_keys,
    new_values,
    head_groups,
    out_weight,
):
    ctx_count = lax.axis_size("ctx")
    position_me = lax.axis_index("ctx")
    row_count, heads_here, head_width = queries.shape
    slot_count = cache_keys.shape[1]
    spans_here = row_count // SPAN
    inverse = 1.0 / math.sqrt(head_width)
    codes = jnp.arange(scale_table.shape[1], dtype=jnp.int32)
    one_hot = scale_index[:, :, None] == codes[None, None, :]
    if ctx_count == 4 and lax.axis_size("head") % 4 == 0:
        expanded = jnp.repeat(
            jnp.sum(
                jnp.where(one_hot[None], scale_table[:, None, None, :], 0.0), axis=3
            ),
            slot_count // scale_index.shape[1],
            axis=2,
        )
        meta = jnp.concatenate(
            [
                expanded[0] * (inverse * LOG2E),
                expanded[1],
                jnp.broadcast_to(hist_lengths.astype(jnp.float32)[:, None], (8, slot_count)),
            ],
            axis=0,
        )
        flat = gather_and_attend(
            jnp.transpose(queries, (1, 0, 2)),
            cache_keys,
            jnp.transpose(cache_values, (0, 2, 1)),
            meta[:, None, :],
            span_offsets,
            head_groups,
            jnp.transpose(new_keys, (1, 0, 2)),
            jnp.transpose(new_values, (1, 2, 0)),
        )
        return project_and_reduce(flat, out_weight)
    one_hot = one_hot.astype(jnp.float32)
    block_scales = jnp.einsum("kbn,tn->tkb", one_hot, scale_table, precision=lax.Precision.HIGHEST)
    slot_scales = jnp.repeat(block_scales, slot_count // scale_index.shape[1], axis=2)
    head_scales = jnp.take(slot_scales, head_groups, axis=1)
    per_block_key_scales = head_scales[0] * inverse
    value_scales = head_scales[1]
    keys_here = jnp.take(cache_keys, head_groups, axis=0)
    values_here = jnp.take(cache_values, head_groups, axis=0)
    start_slot = entering(hist_lengths, "ctx", add_counts, jnp.zeros_like(hist_lengths))
    slot_ids = jnp.arange(slot_count, dtype=jnp.int32)
    live = slot_ids < hist_lengths[0]
    positions = start_slot[0] + slot_ids

    def block_partial(query_block, source):
        offsets = lax.dynamic_slice_in_dim(span_offsets, source * spans_here, spans_here)
        limits = jnp.repeat(offsets, SPAN)
        visible = live[None, :] & (positions[None, :] < limits[:, None])
        unscaled_scores = jnp.einsum(
            "rhd,hsd->hrs", query_block, keys_here, preferred_element_type=jnp.float32
        )
        logit_scores = unscaled_scores * per_block_key_scales[:, None, :]
        masked = jnp.where(visible[None], logit_scores, floor_score)
        block_top = jnp.max(masked, axis=2)
        block_expo = jnp.where(visible[None], jnp.exp(masked - block_top[:, :, None]), 0.0)
        any_visible = jnp.any(visible, axis=1)
        block_total = jnp.where(any_visible[None, :], jnp.sum(block_expo, axis=2), 1.0)
        weights = (block_expo * value_scales[:, None, :]).astype(jnp.bfloat16)
        mixed = jnp.einsum("hrs,hsd->rhd", weights, values_here, preferred_element_type=jnp.float32)
        mixed = mixed / jnp.transpose(block_total)[:, :, None]
        block_lse = jnp.where(any_visible[None, :], block_top + jnp.log(block_total), floor_score)
        return (mixed.astype(jnp.bfloat16), block_lse)

    def record(parts, lses, source, query_block):
        part, block_lse = block_partial(query_block, source)
        parts = lax.dynamic_update_index_in_dim(parts, part, source, 0)
        lses = lax.dynamic_update_index_in_dim(lses, block_lse, source, 0)
        return (parts, lses)

    def forward(query_block):
        return passed_along(query_block, "ctx", 1)

    parts = jnp.zeros((ctx_count, row_count, heads_here, head_width), jnp.bfloat16)
    lses = jnp.full((ctx_count, heads_here, row_count), floor_score, jnp.float32)
    parts, lses = record(parts, lses, position_me, queries)

    def one_turn(turn, carry):
        travelling, parts_now, lses_now = carry
        travelling = forward(travelling)
        parts_now, lses_now = record(
            parts_now, lses_now, (position_me - turn) % ctx_count, travelling
        )
        return (travelling, parts_now, lses_now)

    travelling, parts, lses = lax.fori_loop(1, ctx_count, one_turn, (queries, parts, lses))
    query_spans = queries.reshape(spans_here, SPAN, heads_here, head_width)
    fresh_keys = jnp.take(new_keys, head_groups, axis=1).reshape(
        spans_here, SPAN, heads_here, head_width
    )
    fresh_values = jnp.take(new_values, head_groups, axis=1).reshape(
        spans_here, SPAN, heads_here, head_width
    )
    causal = jnp.arange(SPAN)[:, None] >= jnp.arange(SPAN)[None, :]
    fresh_raw = (
        jnp.einsum("crhd,cshd->chrs", query_spans, fresh_keys, preferred_element_type=jnp.float32)
        * inverse
    )
    fresh_masked = jnp.where(causal[None, None], fresh_raw, floor_score)
    fresh_top = jnp.max(fresh_masked, axis=3)
    fresh_expo = jnp.where(causal[None, None], jnp.exp(fresh_masked - fresh_top[..., None]), 0.0)
    fresh_total = jnp.sum(fresh_expo, axis=3)
    fresh_weights = fresh_expo.astype(jnp.bfloat16)
    fresh = jnp.einsum(
        "chrs,cshd->crhd", fresh_weights, fresh_values, preferred_element_type=jnp.float32
    )
    fresh = fresh / jnp.transpose(fresh_total, (0, 2, 1))[..., None]
    fresh = fresh.reshape(row_count, heads_here, head_width)
    fresh_lse = jnp.transpose(fresh_top + jnp.log(fresh_total), (1, 0, 2)).reshape(
        heads_here, row_count
    )
    home_parts, home_lses = (
        lax.all_to_all(parts.astype(jnp.float32), "ctx", split_axis=0, concat_axis=0, tiled=True),
        lax.all_to_all(lses, "ctx", split_axis=0, concat_axis=0, tiled=True),
    )
    peak = jnp.maximum(jnp.max(home_lses, axis=0), fresh_lse)
    block_weight = jnp.exp(home_lses - peak[None])
    fresh_weight = jnp.exp(fresh_lse - peak)
    numer_all = jnp.transpose(fresh_weight)[:, :, None] * fresh
    numer_all = numer_all + jnp.sum(
        jnp.transpose(block_weight, (0, 2, 1))[..., None] * home_parts, axis=0
    )
    denom_all = fresh_weight + jnp.sum(block_weight, axis=0)
    attended = (numer_all / jnp.transpose(denom_all)[:, :, None]).astype(jnp.bfloat16)
    flat = attended.reshape(row_count, heads_here * head_width)
    return project_and_reduce(flat, out_weight)


def solution(mesh):
    placed = (
        P("ctx", "head", None),
        P(None, "ctx", None),
        P(None, "ctx", None),
        P(None, "ctx"),
        P(),
        P("ctx"),
        P(),
        P("ctx", None, None),
        P("ctx", None, None),
        P("head"),
        P("head", None),
    )
    return jax.shard_map(
        shards, mesh=mesh, in_specs=placed, out_specs=P("ctx", "head"), check_vma=False
    )
```

```python
import math

import jax
import jax.numpy as jnp
from jax import lax
from jax.experimental import pallas as pl
from jax.experimental.pallas import tpu as pltpu
from jax.sharding import PartitionSpec as P

MESH = pl.DeviceIdType.MESH
LOG2E = math.log2(math.e)

SPAN = 128


floor_score = -1e30


def entering(part, axis, combine, identity):
    place = lax.axis_index(axis)
    gathered = lax.all_gather(part, axis)
    state = jnp.zeros_like(part) + jnp.asarray(identity, part.dtype)

    def one(hop, state):
        return combine(state, lax.dynamic_index_in_dim(gathered, hop, 0, False))

    return lax.fori_loop(0, place, one, state)


def passed_along(value, axis, steps):
    count = lax.axis_size(axis)
    pairs = [(source, (source + steps) % count) for source in range(count)]
    return lax.ppermute(value, axis, pairs)


def add_counts(earlier, later):
    return earlier + later


def project_and_reduce(flat, out_weight):
    heads = lax.axis_size("head")
    planes = heads // 2
    rows, depth = flat.shape
    width = out_weight.shape[1] // heads
    pieces = 8
    flying = 4
    piece = rows // pieces
    tile = 256
    slots = 4
    order = [
        sorted(range(planes), key=lambda d, z=z: (-abs(d - z), d if z < planes // 2 else -d))
        for z in range(planes)
    ]

    def kernel(
        flat_ref, weight_ref, out_ref, weights, own, pair_out, pair_in,
        up_out, up_in, down_out, down_in,
        weight_sem, pair_send, pair_recv, up_send, up_recv, down_send, down_recv,
    ):
        me = lax.axis_index("head")
        plane = me // 2
        core = me % 2
        sibling = {"head": 2 * plane + 1 - core}
        above = {"head": me + 2}
        below = {"head": me - 2}
        has_above = plane < planes - 1
        has_below = plane > 0

        def target(step):
            d = jnp.int32(order[0][step])
            for z in range(1, planes):
                d = jnp.where(plane == z, order[z][step], d)
            return d

        targets = [target(step) for step in range(planes)]
        both_ways = (targets[0] > plane) != (targets[min(1, planes - 1)] > plane)
        blocks = []
        for d in targets:
            blocks += [2 * d + 1 - core, 2 * d + core]

        def fetch(i):
            column = pl.multiple_of(blocks[i] * width, width)
            return pltpu.make_async_copy(
                weight_ref.at[:, pl.ds(column, width)], weights.at[i % slots], weight_sem.at[i % slots]
            )

        for i in range(slots - 1):
            fetch(i).start()

        barrier = pltpu.get_barrier_semaphore()
        pl.semaphore_signal(barrier, inc=1, device_id=sibling, device_id_type=MESH)

        @pl.when(has_above)
        def _():
            pl.semaphore_signal(barrier, inc=1, device_id=above, device_id_type=MESH)

        @pl.when(has_below)
        def _():
            pl.semaphore_signal(barrier, inc=1, device_id=below, device_id_type=MESH)

        pl.semaphore_wait(barrier, 1 + has_above.astype(jnp.int32) + has_below.astype(jnp.int32))

        def to_sibling(d):
            return pltpu.make_async_remote_copy(
                src_ref=pair_out.at[d], dst_ref=pair_in.at[d],
                send_sem=pair_send.at[d], recv_sem=pair_recv.at[d],
                device_id=sibling, device_id_type=MESH,
            )

        def upward(d, p):
            return pltpu.make_async_remote_copy(
                src_ref=up_out.at[d, p], dst_ref=up_in.at[d, p],
                send_sem=up_send.at[d, p], recv_sem=up_recv.at[d, p],
                device_id=above, device_id_type=MESH,
            )

        def downward(d, p):
            return pltpu.make_async_remote_copy(
                src_ref=down_out.at[d, p], dst_ref=down_in.at[d, p],
                send_sem=down_send.at[d, p], recv_sem=down_recv.at[d, p],
                device_id=below, device_id_type=MESH,
            )

        def multiply(i, store):
            if i + slots - 1 < len(blocks):
                fetch(i + slots - 1).start()
            fetch(i).wait()

            @pl.loop(0, width // tile)
            def _(t):
                columns = pl.ds(pl.multiple_of(t * tile, tile), tile)
                store(
                    columns,
                    jnp.dot(
                        flat_ref[...], weights[i % slots, :, columns],
                        preferred_element_type=jnp.float32,
                    ),
                )

        def combine(begin, end, place_of):
            @pl.loop(begin, end)
            def _(i):
                d, p = place_of(i)
                span = pl.ds(pl.multiple_of(p * piece, piece), piece)

                @pl.when(d > plane)
                def _():
                    total = own[d, span] + pair_in[d, span].astype(jnp.float32)

                    @pl.when(has_below)
                    def _():
                        upward(d, p).wait_recv()
                        up_out[d, p] = (total + up_in[d, p].astype(jnp.float32)).astype(jnp.bfloat16)

                    @pl.when(jnp.logical_not(has_below))
                    def _():
                        up_out[d, p] = total.astype(jnp.bfloat16)

                    @pl.when(p >= flying)
                    def _():
                        upward(d, p - flying).wait_send()

                    @pl.when((p < flying) & (d < planes - 1))
                    def _():
                        upward(d + 1, p + pieces - flying).wait_send()

                    upward(d, p).start()

                @pl.when(d < plane)
                def _():
                    total = own[d, span] + pair_in[d, span].astype(jnp.float32)

                    @pl.when(has_above)
                    def _():
                        downward(d, p).wait_recv()
                        down_out[d, p] = (total + down_in[d, p].astype(jnp.float32)).astype(
                            jnp.bfloat16
                        )

                    @pl.when(jnp.logical_not(has_above))
                    def _():
                        down_out[d, p] = total.astype(jnp.bfloat16)

                    @pl.when(p >= flying)
                    def _():
                        downward(d, p - flying).wait_send()

                    @pl.when((p < flying) & (d > 0))
                    def _():
                        downward(d - 1, p + pieces - flying).wait_send()

                    downward(d, p).start()

                @pl.when(d == plane)
                def _():
                    own[d, span] = own[d, span] + pair_in[d, span].astype(jnp.float32)

                    @pl.when(has_below)
                    def _():
                        upward(d, p).wait_recv()
                        own[d, span] = own[d, span] + up_in[d, p].astype(jnp.float32)

                    @pl.when(has_above)
                    def _():
                        downward(d, p).wait_recv()
                        own[d, span] = own[d, span] + down_in[d, p].astype(jnp.float32)

                    out_ref[span] = own[d, span].astype(jnp.bfloat16)

        for step in range(planes):
            d = targets[step]

            def to_pair(columns, value, d=d):
                pair_out[d, :, columns] = value.astype(jnp.bfloat16)

            def to_own(columns, value, d=d):
                own[d, :, columns] = value

            multiply(2 * step, to_pair)
            to_sibling(d).start()
            multiply(2 * step + 1, to_own)
            to_sibling(d).wait_recv()
            if planes < 2 or step > 1:
                combine(0, pieces, lambda i, d=d: (d, i))
            elif step == 0:
                early = jnp.where(both_ways, 0, flying)
                combine(0, early, lambda i, d=d: (d, i))
            else:
                before = targets[0]

                def in_turn(i, d=d):
                    later = jnp.where(both_ways, i % 2, i // pieces)
                    p = jnp.where(both_ways, i // 2, i % pieces)
                    return jnp.where(later == 1, d, before), p

                combine(early, 2 * pieces, in_turn)

        for d in targets:
            to_sibling(d).wait_send()

        @pl.loop(pieces - flying, pieces)
        def _(p):
            @pl.when(has_above)
            def _():
                upward(plane + 1, p).wait_send()

            @pl.when(has_below)
            def _():
                downward(plane - 1, p).wait_send()

    block = (planes, rows, width)
    cut = (planes, pieces, piece, width)
    dma = pltpu.SemaphoreType.DMA
    return pl.pallas_call(
        kernel,
        out_shape=jax.ShapeDtypeStruct((rows, width), jnp.bfloat16),
        in_specs=[pl.BlockSpec(memory_space=pltpu.VMEM), pl.BlockSpec(memory_space=pl.ANY)],
        out_specs=pl.BlockSpec(memory_space=pltpu.VMEM),
        scratch_shapes=[
            pltpu.VMEM((slots, depth, width), jnp.bfloat16),
            pltpu.VMEM(block, jnp.float32),
            pltpu.VMEM(block, jnp.bfloat16),
            pltpu.VMEM(block, jnp.bfloat16),
            pltpu.VMEM(cut, jnp.bfloat16),
            pltpu.VMEM(cut, jnp.bfloat16),
            pltpu.VMEM(cut, jnp.bfloat16),
            pltpu.VMEM(cut, jnp.bfloat16),
            dma((slots,)),
            dma((planes,)),
            dma((planes,)),
            dma((planes, pieces)),
            dma((planes, pieces)),
            dma((planes, pieces)),
            dma((planes, pieces)),
        ],
        compiler_params=pltpu.CompilerParams(
            collective_id=1, has_side_effects=True, vmem_limit_bytes=56 * 1024 * 1024
        ),
        cost_estimate=pl.CostEstimate(
            flops=2 * rows * depth * width * heads,
            bytes_accessed=2 * depth * width * heads,
            transcendentals=0,
        ),
        name="project_and_reduce",
    )(flat, out_weight)


def gather_and_attend(queries, keys, values, meta, offsets, groups, fresh_keys, fresh_values):
    heads_here, row_count, head_width = queries.shape
    group_count, slot_count, _ = keys.shape
    half = slot_count // 2
    near = group_count // 2
    spans_here = row_count // SPAN
    factor = LOG2E / math.sqrt(head_width)

    def kernel(
        offsets_ref, groups_ref, q_ref, k_ref, v_ref, meta_ref, fk_ref, fv_ref, out_ref,
        xf_k, xf_v, xs_k, xs_v, yf_k, yf_v, ys_k, ys_v, dn_k, dn_v, df_k, df_v,
        meta_x, meta_y, meta_d, bias, top, total, mixed,
        send, recv, meta_send, meta_recv,
    ):
        me = lax.axis_index("ctx")
        head = lax.axis_index("head")
        plane = head // 2
        core = head % 2
        parity = plane % 2
        x_place = me + 1 - 2 * (me % 2)
        y_place = (me + 2) % 4
        d_place = 3 - me
        to_x, to_y, to_d = {"ctx": x_place}, {"ctx": y_place}, {"ctx": d_place}
        sibling = {"head": 2 * plane + 1 - core}
        partner = {"head": head + 2 - 4 * parity}
        barrier = pltpu.get_barrier_semaphore()
        for device in (to_x, to_y, to_d, sibling, partner):
            pl.semaphore_signal(barrier, inc=1, device_id=device, device_id_type=MESH)
        pl.semaphore_wait(barrier, 5)

        mine = pl.ds(core * near, near)
        low = pl.ds(core * near, near // 2)
        high = pl.ds(core * near + near // 2, near // 2)
        first = pl.multiple_of(parity * half, 128)
        second = pl.multiple_of((1 - parity) * half, 128)
        started = []

        def copy(source, target, device):
            i = len(started)
            made = pltpu.make_async_remote_copy(
                src_ref=source, dst_ref=target, send_sem=send.at[i], recv_sem=recv.at[i],
                device_id=device, device_id_type=MESH,
            )
            made.start()
            started.append(made)
            return made

        meta_copies = []
        for i, (target, device) in enumerate(((meta_x, to_x), (meta_y, to_y), (meta_d, to_d))):
            made = pltpu.make_async_remote_copy(
                src_ref=meta_ref, dst_ref=target, send_sem=meta_send.at[i], recv_sem=meta_recv.at[i],
                device_id=device, device_id_type=MESH,
            )
            made.start()
            meta_copies.append(made)

        def own(ref, offset):
            slots = pl.ds(offset, half)
            return ref.at[mine, slots] if ref is k_ref else ref.at[mine, :, slots]

        firsts = [
            copy(own(ref, first), target.at[mine], device)
            for ref, tx, ty in ((k_ref, xf_k, yf_k), (v_ref, xf_v, yf_v))
            for target, device in ((tx, to_x), (ty, to_y))
        ]

        def fresh_head(h, carry):
            g = groups_ref[h]
            for t in range(spans_here):
                span = pl.ds(t * SPAN, SPAN)
                scores = lax.dot_general(
                    fk_ref[g, span], q_ref[h, span], (((1,), (1,)), ((), ())),
                    preferred_element_type=jnp.float32,
                ) * factor
                causal = lax.broadcasted_iota(jnp.int32, scores.shape, 1) >= lax.broadcasted_iota(
                    jnp.int32, scores.shape, 0
                )
                scores = jnp.where(causal, scores, floor_score)
                largest = jnp.max(scores, axis=0, keepdims=True)
                expo = jnp.exp2(scores - largest)
                top[h, :, span] = largest
                total[h, :, span] = jnp.sum(expo, axis=0, keepdims=True)
                mixed[h, :, span] = jnp.dot(
                    fv_ref[g, :, span], expo.astype(jnp.bfloat16),
                    preferred_element_type=jnp.float32,
                )
            return carry

        lax.fori_loop(0, heads_here, fresh_head, 0, unroll=2)
        for made in meta_copies:
            made.wait_recv()

        places = ((me, meta_ref), (x_place, meta_x), (y_place, meta_y), (d_place, meta_d))
        slot_ids = lax.broadcasted_iota(jnp.int32, (slot_count, SPAN), 0)
        lengths = [
            m[2 * group_count, :, pl.ds(0, SPAN)].astype(jnp.int32) for _, m in places
        ]
        for b, (place, _) in enumerate(places):
            start = jnp.zeros((1, SPAN), jnp.int32)
            for (other, _), length in zip(places, lengths):
                start = start + jnp.where(other < place, length, 0)
            for t in range(spans_here):
                limit = jnp.minimum(lengths[b], offsets_ref[me * spans_here + t] - start)
                bias[b, :, pl.ds(t * SPAN, SPAN)] = jnp.where(slot_ids < limit, 0.0, floor_score)

        def attend(b, offset, size, keys_of, values_of):
            meta_of = places[b][1]

            def scales(row, j):
                part = meta_of[row, :, pl.ds(offset + j * SPAN, SPAN)]
                return jnp.concatenate([part] * spans_here, axis=1)

            def one(h, carry):
                g = groups_ref[h]
                raw = lax.dot_general(
                    keys_of(g), q_ref[h], (((1,), (1,)), ((), ())),
                    preferred_element_type=jnp.float32,
                )
                scores = [
                    raw[j * SPAN:(j + 1) * SPAN] * scales(g, j)
                    + bias[b, pl.ds(offset + j * SPAN, SPAN), :]
                    for j in range(size // SPAN)
                ]
                before = top[h]
                largest = before
                for score in scores:
                    largest = jnp.maximum(largest, jnp.max(score, axis=0, keepdims=True))
                keep = jnp.exp2(before - largest)
                added = total[h] * keep
                weights = []
                for j, score in enumerate(scores):
                    expo = jnp.exp2(score - largest)
                    added = added + jnp.sum(expo, axis=0, keepdims=True)
                    weights.append((expo * scales(g + group_count, j)).astype(jnp.bfloat16))
                top[h] = largest
                total[h] = added
                mixed[h] = mixed[h] * keep + jnp.dot(
                    values_of(g), jnp.concatenate(weights, axis=0),
                    preferred_element_type=jnp.float32,
                )
                return carry

            lax.fori_loop(0, heads_here, one, 0, unroll=2)

        def attend_ref(b, offset, k, v):
            attend(b, offset, half, lambda g: k[g], lambda g: v[g])

        def attend_own(offset):
            slots = pl.ds(offset, half)
            attend(0, offset, half, lambda g: k_ref[g, slots], lambda g: v_ref[g, :, slots])

        attend_own(0)

        def share(pairs):
            return [copy(ref.at[part], ref.at[part], sibling) for ref, part in pairs]

        def arrived(copies):
            for made in copies:
                made.wait_recv()

        arrived(firsts)
        relays = [
            copy(source.at[part], target.at[part], device)
            for source, target, part, device in (
                (xf_k, dn_k, low, to_y), (yf_k, dn_k, high, to_x),
                (xf_v, dn_v, low, to_y), (yf_v, dn_v, high, to_x),
            )
        ]
        first_shared = share([(xf_k, mine), (xf_v, mine), (yf_k, mine), (yf_v, mine)])
        attend_own(half)
        seconds = [
            copy(own(ref, second), target.at[mine], device)
            for ref, tx, ty in ((k_ref, xs_k, ys_k), (v_ref, xs_v, ys_v))
            for target, device in ((tx, to_x), (ty, to_y))
        ]
        arrived(relays)
        across = [
            copy(source.at[part], target.at[part], partner)
            for source, target in ((dn_k, df_k), (dn_v, df_v))
            for part in (low, high)
        ]
        near_shared = share([(dn_k, mine), (dn_v, mine)])
        arrived(first_shared)
        attend_ref(1, first, xf_k, xf_v)
        attend_ref(2, first, yf_k, yf_v)
        arrived(seconds)
        second_shared = share([(xs_k, mine), (xs_v, mine), (ys_k, mine), (ys_v, mine)])
        arrived(near_shared)
        attend_ref(3, first, dn_k, dn_v)
        arrived(across)
        far_shared = share([(df_k, mine), (df_v, mine)])
        arrived(second_shared)
        attend_ref(1, second, xs_k, xs_v)
        attend_ref(2, second, ys_k, ys_v)
        arrived(far_shared)
        attend_ref(3, second, df_k, df_v)

        def finish(h, carry):
            columns = pl.ds(pl.multiple_of(h * head_width, head_width), head_width)
            out_ref[:, columns] = jnp.transpose(mixed[h] / total[h]).astype(jnp.bfloat16)
            return carry

        lax.fori_loop(0, heads_here, finish, 0)
        for made in started + meta_copies:
            made.wait_send()

    key_chunk = pltpu.VMEM((group_count, half, head_width), jnp.bfloat16)
    value_chunk = pltpu.VMEM((group_count, head_width, half), jnp.bfloat16)
    table = pltpu.VMEM(meta.shape, jnp.float32)
    dma = pltpu.SemaphoreType.DMA
    copies = 4 + 4 + 4 + 4 + 4 + 2 + 4 + 2
    whole = pl.BlockSpec(memory_space=pltpu.VMEM)
    scalar = pl.BlockSpec(memory_space=pltpu.SMEM)
    return pl.pallas_call(
        kernel,
        out_shape=jax.ShapeDtypeStruct((row_count, heads_here * head_width), jnp.bfloat16),
        in_specs=[scalar, scalar] + [whole] * 6,
        out_specs=whole,
        scratch_shapes=[key_chunk, value_chunk] * 6
        + [table] * 3
        + [
            pltpu.VMEM((4, slot_count, row_count), jnp.float32),
            pltpu.VMEM((heads_here, 1, row_count), jnp.float32),
            pltpu.VMEM((heads_here, 1, row_count), jnp.float32),
            pltpu.VMEM((heads_here, head_width, row_count), jnp.float32),
            dma((copies,)),
            dma((copies,)),
            dma((3,)),
            dma((3,)),
        ],
        compiler_params=pltpu.CompilerParams(
            collective_id=2, has_side_effects=True, vmem_limit_bytes=56 * 1024 * 1024
        ),
        cost_estimate=pl.CostEstimate(
            flops=16 * row_count * heads_here * slot_count * head_width,
            bytes_accessed=8 * group_count * slot_count * head_width,
            transcendentals=4 * row_count * heads_here * slot_count,
        ),
        name="gather_and_attend",
    )(offsets, groups, queries, keys, values, meta, fresh_keys, fresh_values)


def shards(
    queries,
    cache_keys,
    cache_values,
    scale_index,
    scale_table,
    hist_lengths,
    span_offsets,
    new_keys,
    new_values,
    head_groups,
    out_weight,
):
    ctx_count = lax.axis_size("ctx")
    position_me = lax.axis_index("ctx")
    row_count, heads_here, head_width = queries.shape
    slot_count = cache_keys.shape[1]
    spans_here = row_count // SPAN
    inverse = 1.0 / math.sqrt(head_width)
    codes = jnp.arange(scale_table.shape[1], dtype=jnp.int32)
    one_hot = scale_index[:, :, None] == codes[None, None, :]
    if ctx_count == 4 and lax.axis_size("head") % 4 == 0:
        expanded = jnp.repeat(
            jnp.sum(
                jnp.where(one_hot[None], scale_table[:, None, None, :], 0.0), axis=3
            ),
            slot_count // scale_index.shape[1],
            axis=2,
        )
        meta = jnp.concatenate(
            [
                expanded[0] * (inverse * LOG2E),
                expanded[1],
                jnp.broadcast_to(hist_lengths.astype(jnp.float32)[:, None], (8, slot_count)),
            ],
            axis=0,
        )
        flat = gather_and_attend(
            jnp.transpose(queries, (1, 0, 2)),
            cache_keys,
            jnp.transpose(cache_values, (0, 2, 1)),
            meta[:, None, :],
            span_offsets,
            head_groups,
            jnp.transpose(new_keys, (1, 0, 2)),
            jnp.transpose(new_values, (1, 2, 0)),
        )
        return project_and_reduce(flat, out_weight)
    one_hot = one_hot.astype(jnp.float32)
    block_scales = jnp.einsum("kbn,tn->tkb", one_hot, scale_table, precision=lax.Precision.HIGHEST)
    slot_scales = jnp.repeat(block_scales, slot_count // scale_index.shape[1], axis=2)
    head_scales = jnp.take(slot_scales, head_groups, axis=1)
    per_block_key_scales = head_scales[0] * inverse
    value_scales = head_scales[1]
    keys_here = jnp.take(cache_keys, head_groups, axis=0)
    values_here = jnp.take(cache_values, head_groups, axis=0)
    start_slot = entering(hist_lengths, "ctx", add_counts, jnp.zeros_like(hist_lengths))
    slot_ids = jnp.arange(slot_count, dtype=jnp.int32)
    live = slot_ids < hist_lengths[0]
    positions = start_slot[0] + slot_ids

    def block_partial(query_block, source):
        offsets = lax.dynamic_slice_in_dim(span_offsets, source * spans_here, spans_here)
        limits = jnp.repeat(offsets, SPAN)
        visible = live[None, :] & (positions[None, :] < limits[:, None])
        unscaled_scores = jnp.einsum(
            "rhd,hsd->hrs", query_block, keys_here, preferred_element_type=jnp.float32
        )
        logit_scores = unscaled_scores * per_block_key_scales[:, None, :]
        masked = jnp.where(visible[None], logit_scores, floor_score)
        block_top = jnp.max(masked, axis=2)
        block_expo = jnp.where(visible[None], jnp.exp(masked - block_top[:, :, None]), 0.0)
        any_visible = jnp.any(visible, axis=1)
        block_total = jnp.where(any_visible[None, :], jnp.sum(block_expo, axis=2), 1.0)
        weights = (block_expo * value_scales[:, None, :]).astype(jnp.bfloat16)
        mixed = jnp.einsum("hrs,hsd->rhd", weights, values_here, preferred_element_type=jnp.float32)
        mixed = mixed / jnp.transpose(block_total)[:, :, None]
        block_lse = jnp.where(any_visible[None, :], block_top + jnp.log(block_total), floor_score)
        return (mixed.astype(jnp.bfloat16), block_lse)

    def record(parts, lses, source, query_block):
        part, block_lse = block_partial(query_block, source)
        parts = lax.dynamic_update_index_in_dim(parts, part, source, 0)
        lses = lax.dynamic_update_index_in_dim(lses, block_lse, source, 0)
        return (parts, lses)

    def forward(query_block):
        return passed_along(query_block, "ctx", 1)

    parts = jnp.zeros((ctx_count, row_count, heads_here, head_width), jnp.bfloat16)
    lses = jnp.full((ctx_count, heads_here, row_count), floor_score, jnp.float32)
    parts, lses = record(parts, lses, position_me, queries)

    def one_turn(turn, carry):
        travelling, parts_now, lses_now = carry
        travelling = forward(travelling)
        parts_now, lses_now = record(
            parts_now, lses_now, (position_me - turn) % ctx_count, travelling
        )
        return (travelling, parts_now, lses_now)

    travelling, parts, lses = lax.fori_loop(1, ctx_count, one_turn, (queries, parts, lses))
    query_spans = queries.reshape(spans_here, SPAN, heads_here, head_width)
    fresh_keys = jnp.take(new_keys, head_groups, axis=1).reshape(
        spans_here, SPAN, heads_here, head_width
    )
    fresh_values = jnp.take(new_values, head_groups, axis=1).reshape(
        spans_here, SPAN, heads_here, head_width
    )
    causal = jnp.arange(SPAN)[:, None] >= jnp.arange(SPAN)[None, :]
    fresh_raw = (
        jnp.einsum("crhd,cshd->chrs", query_spans, fresh_keys, preferred_element_type=jnp.float32)
        * inverse
    )
    fresh_masked = jnp.where(causal[None, None], fresh_raw, floor_score)
    fresh_top = jnp.max(fresh_masked, axis=3)
    fresh_expo = jnp.where(causal[None, None], jnp.exp(fresh_masked - fresh_top[..., None]), 0.0)
    fresh_total = jnp.sum(fresh_expo, axis=3)
    fresh_weights = fresh_expo.astype(jnp.bfloat16)
    fresh = jnp.einsum(
        "chrs,cshd->crhd", fresh_weights, fresh_values, preferred_element_type=jnp.float32
    )
    fresh = fresh / jnp.transpose(fresh_total, (0, 2, 1))[..., None]
    fresh = fresh.reshape(row_count, heads_here, head_width)
    fresh_lse = jnp.transpose(fresh_top + jnp.log(fresh_total), (1, 0, 2)).reshape(
        heads_here, row_count
    )
    home_parts, home_lses = (
        lax.all_to_all(parts.astype(jnp.float32), "ctx", split_axis=0, concat_axis=0, tiled=True),
        lax.all_to_all(lses, "ctx", split_axis=0, concat_axis=0, tiled=True),
    )
    peak = jnp.maximum(jnp.max(home_lses, axis=0), fresh_lse)
    block_weight = jnp.exp(home_lses - peak[None])
    fresh_weight = jnp.exp(fresh_lse - peak)
    numer_all = jnp.transpose(fresh_weight)[:, :, None] * fresh
    numer_all = numer_all + jnp.sum(
        jnp.transpose(block_weight, (0, 2, 1))[..., None] * home_parts, axis=0
    )
    denom_all = fresh_weight + jnp.sum(block_weight, axis=0)
    attended = (numer_all / jnp.transpose(denom_all)[:, :, None]).astype(jnp.bfloat16)
    flat = attended.reshape(row_count, heads_here * head_width)
    return project_and_reduce(flat, out_weight)


def solution(mesh):
    placed = (
        P("ctx", "head", None),
        P(None, "ctx", None),
        P(None, "ctx", None),
        P(None, "ctx"),
        P(),
        P("ctx"),
        P(),
        P("ctx", None, None),
        P("ctx", None, None),
        P("head"),
        P("head", None),
    )
    return jax.shard_map(
        shards, mesh=mesh, in_specs=placed, out_specs=P("ctx", "head"), check_vma=False
    )
```

```python
import math

import jax
import jax.numpy as jnp
from jax import lax
from jax.experimental import pallas as pl
from jax.experimental.pallas import tpu as pltpu
from jax.sharding import PartitionSpec as P

MESH = pl.DeviceIdType.MESH
LOG2E = math.log2(math.e)

SPAN = 128


floor_score = -1e30


def entering(part, axis, combine, identity):
    place = lax.axis_index(axis)
    gathered = lax.all_gather(part, axis)
    state = jnp.zeros_like(part) + jnp.asarray(identity, part.dtype)

    def one(hop, state):
        return combine(state, lax.dynamic_index_in_dim(gathered, hop, 0, False))

    return lax.fori_loop(0, place, one, state)


def passed_along(value, axis, steps):
    count = lax.axis_size(axis)
    pairs = [(source, (source + steps) % count) for source in range(count)]
    return lax.ppermute(value, axis, pairs)


def add_counts(earlier, later):
    return earlier + later


def project_and_reduce(flat, out_weight):
    heads = lax.axis_size("head")
    planes = heads // 2
    rows, depth = flat.shape
    width = out_weight.shape[1] // heads
    pieces = 8
    flying = 4
    piece = rows // pieces
    tile = 256
    slots = 4
    order = [
        sorted(range(planes), key=lambda d, z=z: (-abs(d - z), d if z < planes // 2 else -d))
        for z in range(planes)
    ]

    def kernel(
        flat_ref, weight_ref, out_ref, weights, own, pair_out, pair_in,
        up_out, up_in, down_out, down_in,
        weight_sem, pair_send, pair_recv, up_send, up_recv, down_send, down_recv,
    ):
        me = lax.axis_index("head")
        plane = me // 2
        core = me % 2
        sibling = {"head": 2 * plane + 1 - core}
        above = {"head": me + 2}
        below = {"head": me - 2}
        has_above = plane < planes - 1
        has_below = plane > 0

        def target(step):
            d = jnp.int32(order[0][step])
            for z in range(1, planes):
                d = jnp.where(plane == z, order[z][step], d)
            return d

        targets = [target(step) for step in range(planes)]
        blocks = []
        for d in targets:
            blocks += [2 * d + 1 - core, 2 * d + core]

        def fetch(i):
            column = pl.multiple_of(blocks[i] * width, width)
            return pltpu.make_async_copy(
                weight_ref.at[:, pl.ds(column, width)], weights.at[i % slots], weight_sem.at[i % slots]
            )

        for i in range(slots - 1):
            fetch(i).start()

        barrier = pltpu.get_barrier_semaphore()
        pl.semaphore_signal(barrier, inc=1, device_id=sibling, device_id_type=MESH)

        @pl.when(has_above)
        def _():
            pl.semaphore_signal(barrier, inc=1, device_id=above, device_id_type=MESH)

        @pl.when(has_below)
        def _():
            pl.semaphore_signal(barrier, inc=1, device_id=below, device_id_type=MESH)

        pl.semaphore_wait(barrier, 1 + has_above.astype(jnp.int32) + has_below.astype(jnp.int32))

        def to_sibling(d):
            return pltpu.make_async_remote_copy(
                src_ref=pair_out.at[d], dst_ref=pair_in.at[d],
                send_sem=pair_send.at[d], recv_sem=pair_recv.at[d],
                device_id=sibling, device_id_type=MESH,
            )

        def upward(d, p):
            return pltpu.make_async_remote_copy(
                src_ref=up_out.at[d, p], dst_ref=up_in.at[d, p],
                send_sem=up_send.at[d, p], recv_sem=up_recv.at[d, p],
                device_id=above, device_id_type=MESH,
            )

        def downward(d, p):
            return pltpu.make_async_remote_copy(
                src_ref=down_out.at[d, p], dst_ref=down_in.at[d, p],
                send_sem=down_send.at[d, p], recv_sem=down_recv.at[d, p],
                device_id=below, device_id_type=MESH,
            )

        def multiply(i, store):
            if i + slots - 1 < len(blocks):
                fetch(i + slots - 1).start()
            fetch(i).wait()

            @pl.loop(0, width // tile)
            def _(t):
                columns = pl.ds(pl.multiple_of(t * tile, tile), tile)
                store(
                    columns,
                    jnp.dot(
                        flat_ref[...], weights[i % slots, :, columns],
                        preferred_element_type=jnp.float32,
                    ),
                )

        def combine(d):
            to_sibling(d).wait_recv()

            @pl.loop(0, pieces)
            def _(p):
                span = pl.ds(pl.multiple_of(p * piece, piece), piece)

                @pl.when(d > plane)
                def _():
                    total = own[d, span] + pair_in[d, span].astype(jnp.float32)

                    @pl.when(has_below)
                    def _():
                        upward(d, p).wait_recv()
                        up_out[d, p] = (total + up_in[d, p].astype(jnp.float32)).astype(jnp.bfloat16)

                    @pl.when(jnp.logical_not(has_below))
                    def _():
                        up_out[d, p] = total.astype(jnp.bfloat16)

                    @pl.when(p >= flying)
                    def _():
                        upward(d, p - flying).wait_send()

                    @pl.when((p < flying) & (d < planes - 1))
                    def _():
                        upward(d + 1, p + pieces - flying).wait_send()

                    upward(d, p).start()

                @pl.when(d < plane)
                def _():
                    total = own[d, span] + pair_in[d, span].astype(jnp.float32)

                    @pl.when(has_above)
                    def _():
                        downward(d, p).wait_recv()
                        down_out[d, p] = (total + down_in[d, p].astype(jnp.float32)).astype(
                            jnp.bfloat16
                        )

                    @pl.when(jnp.logical_not(has_above))
                    def _():
                        down_out[d, p] = total.astype(jnp.bfloat16)

                    @pl.when(p >= flying)
                    def _():
                        downward(d, p - flying).wait_send()

                    @pl.when((p < flying) & (d > 0))
                    def _():
                        downward(d - 1, p + pieces - flying).wait_send()

                    downward(d, p).start()

                @pl.when(d == plane)
                def _():
                    own[d, span] = own[d, span] + pair_in[d, span].astype(jnp.float32)

                    @pl.when(has_below)
                    def _():
                        upward(d, p).wait_recv()
                        own[d, span] = own[d, span] + up_in[d, p].astype(jnp.float32)

                    @pl.when(has_above)
                    def _():
                        downward(d, p).wait_recv()
                        own[d, span] = own[d, span] + down_in[d, p].astype(jnp.float32)

                    out_ref[span] = own[d, span].astype(jnp.bfloat16)

        for step in range(planes):
            d = targets[step]

            def to_pair(columns, value, d=d):
                pair_out[d, :, columns] = value.astype(jnp.bfloat16)

            def to_own(columns, value, d=d):
                own[d, :, columns] = value

            multiply(2 * step, to_pair)
            to_sibling(d).start()
            multiply(2 * step + 1, to_own)
            combine(d)

        for d in targets:
            to_sibling(d).wait_send()

        @pl.loop(pieces - flying, pieces)
        def _(p):
            @pl.when(has_above)
            def _():
                upward(plane + 1, p).wait_send()

            @pl.when(has_below)
            def _():
                downward(plane - 1, p).wait_send()

    block = (planes, rows, width)
    cut = (planes, pieces, piece, width)
    dma = pltpu.SemaphoreType.DMA
    return pl.pallas_call(
        kernel,
        out_shape=jax.ShapeDtypeStruct((rows, width), jnp.bfloat16),
        in_specs=[pl.BlockSpec(memory_space=pltpu.VMEM), pl.BlockSpec(memory_space=pl.ANY)],
        out_specs=pl.BlockSpec(memory_space=pltpu.VMEM),
        scratch_shapes=[
            pltpu.VMEM((slots, depth, width), jnp.bfloat16),
            pltpu.VMEM(block, jnp.float32),
            pltpu.VMEM(block, jnp.bfloat16),
            pltpu.VMEM(block, jnp.bfloat16),
            pltpu.VMEM(cut, jnp.bfloat16),
            pltpu.VMEM(cut, jnp.bfloat16),
            pltpu.VMEM(cut, jnp.bfloat16),
            pltpu.VMEM(cut, jnp.bfloat16),
            dma((slots,)),
            dma((planes,)),
            dma((planes,)),
            dma((planes, pieces)),
            dma((planes, pieces)),
            dma((planes, pieces)),
            dma((planes, pieces)),
        ],
        compiler_params=pltpu.CompilerParams(
            collective_id=1, has_side_effects=True, vmem_limit_bytes=56 * 1024 * 1024
        ),
        cost_estimate=pl.CostEstimate(
            flops=2 * rows * depth * width * heads,
            bytes_accessed=2 * depth * width * heads,
            transcendentals=0,
        ),
        name="project_and_reduce",
    )(flat, out_weight)


def gather_and_attend(queries, keys, values, meta, offsets, groups, fresh_keys, fresh_values):
    heads_here, row_count, head_width = queries.shape
    group_count, slot_count, _ = keys.shape
    half = slot_count // 2
    near = group_count // 2
    spans_here = row_count // SPAN
    factor = LOG2E / math.sqrt(head_width)
    together = math.gcd(heads_here, 4)

    def kernel(
        offsets_ref, groups_ref, q_ref, k_ref, v_ref, meta_ref, fk_ref, fv_ref, out_ref,
        xf_k, xf_v, xs_k, xs_v, yf_k, yf_v, ys_k, ys_v, dn_k, dn_v, df_k, df_v,
        meta_x, meta_y, meta_d, bias, top, total, mixed,
        send, recv, meta_send, meta_recv,
    ):
        me = lax.axis_index("ctx")
        head = lax.axis_index("head")
        plane = head // 2
        core = head % 2
        parity = plane % 2
        x_place = me + 1 - 2 * (me % 2)
        y_place = (me + 2) % 4
        d_place = 3 - me
        to_x, to_y, to_d = {"ctx": x_place}, {"ctx": y_place}, {"ctx": d_place}
        sibling = {"head": 2 * plane + 1 - core}
        partner = {"head": head + 2 - 4 * parity}
        barrier = pltpu.get_barrier_semaphore()
        for device in (to_x, to_y, to_d, sibling, partner):
            pl.semaphore_signal(barrier, inc=1, device_id=device, device_id_type=MESH)
        pl.semaphore_wait(barrier, 5)

        mine = pl.ds(core * near, near)
        low = pl.ds(core * near, near // 2)
        high = pl.ds(core * near + near // 2, near // 2)
        first = pl.multiple_of(parity * half, 128)
        second = pl.multiple_of((1 - parity) * half, 128)
        started = []

        def copy(source, target, device):
            i = len(started)
            made = pltpu.make_async_remote_copy(
                src_ref=source, dst_ref=target, send_sem=send.at[i], recv_sem=recv.at[i],
                device_id=device, device_id_type=MESH,
            )
            made.start()
            started.append(made)
            return made

        meta_copies = []
        for i, (target, device) in enumerate(((meta_x, to_x), (meta_y, to_y), (meta_d, to_d))):
            made = pltpu.make_async_remote_copy(
                src_ref=meta_ref, dst_ref=target, send_sem=meta_send.at[i], recv_sem=meta_recv.at[i],
                device_id=device, device_id_type=MESH,
            )
            made.start()
            meta_copies.append(made)

        def own(ref, offset):
            slots = pl.ds(offset, half)
            return ref.at[mine, slots] if ref is k_ref else ref.at[mine, :, slots]

        firsts = [
            copy(own(ref, first), target.at[mine], device)
            for ref, tx, ty in ((k_ref, xf_k, yf_k), (v_ref, xf_v, yf_v))
            for target, device in ((tx, to_x), (ty, to_y))
        ]

        def fresh_head(h, carry):
            g = groups_ref[h]
            for t in range(spans_here):
                span = pl.ds(t * SPAN, SPAN)
                scores = lax.dot_general(
                    fk_ref[g, span], q_ref[h, span], (((1,), (1,)), ((), ())),
                    preferred_element_type=jnp.float32,
                ) * factor
                causal = lax.broadcasted_iota(jnp.int32, scores.shape, 1) >= lax.broadcasted_iota(
                    jnp.int32, scores.shape, 0
                )
                scores = jnp.where(causal, scores, floor_score)
                largest = jnp.max(scores, axis=0, keepdims=True)
                expo = jnp.exp2(scores - largest)
                top[h, :, span] = largest
                total[h, :, span] = jnp.sum(expo, axis=0, keepdims=True)
                mixed[h, :, span] = jnp.dot(
                    fv_ref[g, :, span], expo.astype(jnp.bfloat16),
                    preferred_element_type=jnp.float32,
                )
            return carry

        lax.fori_loop(0, heads_here, fresh_head, 0, unroll=2)
        for made in meta_copies:
            made.wait_recv()

        places = ((me, meta_ref), (x_place, meta_x), (y_place, meta_y), (d_place, meta_d))
        slot_ids = lax.broadcasted_iota(jnp.int32, (slot_count, SPAN), 0)
        lengths = [
            m[2 * group_count, :, pl.ds(0, SPAN)].astype(jnp.int32) for _, m in places
        ]
        for b, (place, _) in enumerate(places):
            start = jnp.zeros((1, SPAN), jnp.int32)
            for (other, _), length in zip(places, lengths):
                start = start + jnp.where(other < place, length, 0)
            for t in range(spans_here):
                limit = jnp.minimum(lengths[b], offsets_ref[me * spans_here + t] - start)
                bias[b, :, pl.ds(t * SPAN, SPAN)] = jnp.where(slot_ids < limit, 0.0, floor_score)

        def attend(b, offset, size, keys_of, values_of):
            meta_of = places[b][1]

            def scales(row, j):
                part = meta_of[row, :, pl.ds(offset + j * SPAN, SPAN)]
                return jnp.concatenate([part] * spans_here, axis=1)

            def one(h):
                g = groups_ref[h]
                raw = lax.dot_general(
                    keys_of(g), q_ref[h], (((1,), (1,)), ((), ())),
                    preferred_element_type=jnp.float32,
                )
                scores = [
                    raw[j * SPAN:(j + 1) * SPAN] * scales(g, j)
                    + bias[b, pl.ds(offset + j * SPAN, SPAN), :]
                    for j in range(size // SPAN)
                ]
                before = top[h]
                largest = before
                for score in scores:
                    largest = jnp.maximum(largest, jnp.max(score, axis=0, keepdims=True))
                keep = jnp.exp2(before - largest)
                added = total[h] * keep
                weights = []
                for j, score in enumerate(scores):
                    expo = jnp.exp2(score - largest)
                    added = added + jnp.sum(expo, axis=0, keepdims=True)
                    weights.append((expo * scales(g + group_count, j)).astype(jnp.bfloat16))
                summed = mixed[h] * keep + jnp.dot(
                    values_of(g), jnp.concatenate(weights, axis=0),
                    preferred_element_type=jnp.float32,
                )
                return h, largest, added, summed

            def several(i, carry):
                done = [one(i * together + j) for j in range(together)]
                for h, largest, added, summed in done:
                    top[h] = largest
                    total[h] = added
                    mixed[h] = summed
                return carry

            lax.fori_loop(0, heads_here // together, several, 0)

        def attend_ref(b, offset, k, v):
            attend(b, offset, half, lambda g: k[g], lambda g: v[g])

        def attend_own(offset):
            slots = pl.ds(offset, half)
            attend(0, offset, half, lambda g: k_ref[g, slots], lambda g: v_ref[g, :, slots])

        attend_own(0)

        def share(pairs):
            return [copy(ref.at[part], ref.at[part], sibling) for ref, part in pairs]

        def arrived(copies):
            for made in copies:
                made.wait_recv()

        arrived(firsts)
        relays = [
            copy(source.at[part], target.at[part], device)
            for source, target, part, device in (
                (xf_k, dn_k, low, to_y), (yf_k, dn_k, high, to_x),
                (xf_v, dn_v, low, to_y), (yf_v, dn_v, high, to_x),
            )
        ]
        first_shared = share([(xf_k, mine), (xf_v, mine), (yf_k, mine), (yf_v, mine)])
        attend_own(half)
        seconds = [
            copy(own(ref, second), target.at[mine], device)
            for ref, tx, ty in ((k_ref, xs_k, ys_k), (v_ref, xs_v, ys_v))
            for target, device in ((tx, to_x), (ty, to_y))
        ]
        arrived(relays)
        across = [
            copy(source.at[part], target.at[part], partner)
            for source, target in ((dn_k, df_k), (dn_v, df_v))
            for part in (low, high)
        ]
        near_shared = share([(dn_k, mine), (dn_v, mine)])
        arrived(first_shared)
        attend_ref(1, first, xf_k, xf_v)
        attend_ref(2, first, yf_k, yf_v)
        arrived(seconds)
        second_shared = share([(xs_k, mine), (xs_v, mine), (ys_k, mine), (ys_v, mine)])
        arrived(near_shared)
        attend_ref(3, first, dn_k, dn_v)
        arrived(across)
        far_shared = share([(df_k, mine), (df_v, mine)])
        arrived(second_shared)
        attend_ref(1, second, xs_k, xs_v)
        attend_ref(2, second, ys_k, ys_v)
        arrived(far_shared)
        attend_ref(3, second, df_k, df_v)

        def finish(h, carry):
            columns = pl.ds(pl.multiple_of(h * head_width, head_width), head_width)
            out_ref[:, columns] = jnp.transpose(mixed[h] / total[h]).astype(jnp.bfloat16)
            return carry

        lax.fori_loop(0, heads_here, finish, 0)
        for made in started + meta_copies:
            made.wait_send()

    key_chunk = pltpu.VMEM((group_count, half, head_width), jnp.bfloat16)
    value_chunk = pltpu.VMEM((group_count, head_width, half), jnp.bfloat16)
    table = pltpu.VMEM(meta.shape, jnp.float32)
    dma = pltpu.SemaphoreType.DMA
    copies = 4 + 4 + 4 + 4 + 4 + 2 + 4 + 2
    whole = pl.BlockSpec(memory_space=pltpu.VMEM)
    scalar = pl.BlockSpec(memory_space=pltpu.SMEM)
    return pl.pallas_call(
        kernel,
        out_shape=jax.ShapeDtypeStruct((row_count, heads_here * head_width), jnp.bfloat16),
        in_specs=[scalar, scalar] + [whole] * 6,
        out_specs=whole,
        scratch_shapes=[key_chunk, value_chunk] * 6
        + [table] * 3
        + [
            pltpu.VMEM((4, slot_count, row_count), jnp.float32),
            pltpu.VMEM((heads_here, 1, row_count), jnp.float32),
            pltpu.VMEM((heads_here, 1, row_count), jnp.float32),
            pltpu.VMEM((heads_here, head_width, row_count), jnp.float32),
            dma((copies,)),
            dma((copies,)),
            dma((3,)),
            dma((3,)),
        ],
        compiler_params=pltpu.CompilerParams(
            collective_id=2, has_side_effects=True, vmem_limit_bytes=56 * 1024 * 1024
        ),
        cost_estimate=pl.CostEstimate(
            flops=16 * row_count * heads_here * slot_count * head_width,
            bytes_accessed=8 * group_count * slot_count * head_width,
            transcendentals=4 * row_count * heads_here * slot_count,
        ),
        name="gather_and_attend",
    )(offsets, groups, queries, keys, values, meta, fresh_keys, fresh_values)


def shards(
    queries,
    cache_keys,
    cache_values,
    scale_index,
    scale_table,
    hist_lengths,
    span_offsets,
    new_keys,
    new_values,
    head_groups,
    out_weight,
):
    ctx_count = lax.axis_size("ctx")
    position_me = lax.axis_index("ctx")
    row_count, heads_here, head_width = queries.shape
    slot_count = cache_keys.shape[1]
    spans_here = row_count // SPAN
    inverse = 1.0 / math.sqrt(head_width)
    codes = jnp.arange(scale_table.shape[1], dtype=jnp.int32)
    one_hot = scale_index[:, :, None] == codes[None, None, :]
    if ctx_count == 4 and lax.axis_size("head") % 4 == 0:
        expanded = jnp.repeat(
            jnp.sum(
                jnp.where(one_hot[None], scale_table[:, None, None, :], 0.0), axis=3
            ),
            slot_count // scale_index.shape[1],
            axis=2,
        )
        meta = jnp.concatenate(
            [
                expanded[0] * (inverse * LOG2E),
                expanded[1],
                jnp.broadcast_to(hist_lengths.astype(jnp.float32)[:, None], (8, slot_count)),
            ],
            axis=0,
        )
        flat = gather_and_attend(
            jnp.transpose(queries, (1, 0, 2)),
            cache_keys,
            jnp.transpose(cache_values, (0, 2, 1)),
            meta[:, None, :],
            span_offsets,
            head_groups,
            jnp.transpose(new_keys, (1, 0, 2)),
            jnp.transpose(new_values, (1, 2, 0)),
        )
        return project_and_reduce(flat, out_weight)
    one_hot = one_hot.astype(jnp.float32)
    block_scales = jnp.einsum("kbn,tn->tkb", one_hot, scale_table, precision=lax.Precision.HIGHEST)
    slot_scales = jnp.repeat(block_scales, slot_count // scale_index.shape[1], axis=2)
    head_scales = jnp.take(slot_scales, head_groups, axis=1)
    per_block_key_scales = head_scales[0] * inverse
    value_scales = head_scales[1]
    keys_here = jnp.take(cache_keys, head_groups, axis=0)
    values_here = jnp.take(cache_values, head_groups, axis=0)
    start_slot = entering(hist_lengths, "ctx", add_counts, jnp.zeros_like(hist_lengths))
    slot_ids = jnp.arange(slot_count, dtype=jnp.int32)
    live = slot_ids < hist_lengths[0]
    positions = start_slot[0] + slot_ids

    def block_partial(query_block, source):
        offsets = lax.dynamic_slice_in_dim(span_offsets, source * spans_here, spans_here)
        limits = jnp.repeat(offsets, SPAN)
        visible = live[None, :] & (positions[None, :] < limits[:, None])
        unscaled_scores = jnp.einsum(
            "rhd,hsd->hrs", query_block, keys_here, preferred_element_type=jnp.float32
        )
        logit_scores = unscaled_scores * per_block_key_scales[:, None, :]
        masked = jnp.where(visible[None], logit_scores, floor_score)
        block_top = jnp.max(masked, axis=2)
        block_expo = jnp.where(visible[None], jnp.exp(masked - block_top[:, :, None]), 0.0)
        any_visible = jnp.any(visible, axis=1)
        block_total = jnp.where(any_visible[None, :], jnp.sum(block_expo, axis=2), 1.0)
        weights = (block_expo * value_scales[:, None, :]).astype(jnp.bfloat16)
        mixed = jnp.einsum("hrs,hsd->rhd", weights, values_here, preferred_element_type=jnp.float32)
        mixed = mixed / jnp.transpose(block_total)[:, :, None]
        block_lse = jnp.where(any_visible[None, :], block_top + jnp.log(block_total), floor_score)
        return (mixed.astype(jnp.bfloat16), block_lse)

    def record(parts, lses, source, query_block):
        part, block_lse = block_partial(query_block, source)
        parts = lax.dynamic_update_index_in_dim(parts, part, source, 0)
        lses = lax.dynamic_update_index_in_dim(lses, block_lse, source, 0)
        return (parts, lses)

    def forward(query_block):
        return passed_along(query_block, "ctx", 1)

    parts = jnp.zeros((ctx_count, row_count, heads_here, head_width), jnp.bfloat16)
    lses = jnp.full((ctx_count, heads_here, row_count), floor_score, jnp.float32)
    parts, lses = record(parts, lses, position_me, queries)

    def one_turn(turn, carry):
        travelling, parts_now, lses_now = carry
        travelling = forward(travelling)
        parts_now, lses_now = record(
            parts_now, lses_now, (position_me - turn) % ctx_count, travelling
        )
        return (travelling, parts_now, lses_now)

    travelling, parts, lses = lax.fori_loop(1, ctx_count, one_turn, (queries, parts, lses))
    query_spans = queries.reshape(spans_here, SPAN, heads_here, head_width)
    fresh_keys = jnp.take(new_keys, head_groups, axis=1).reshape(
        spans_here, SPAN, heads_here, head_width
    )
    fresh_values = jnp.take(new_values, head_groups, axis=1).reshape(
        spans_here, SPAN, heads_here, head_width
    )
    causal = jnp.arange(SPAN)[:, None] >= jnp.arange(SPAN)[None, :]
    fresh_raw = (
        jnp.einsum("crhd,cshd->chrs", query_spans, fresh_keys, preferred_element_type=jnp.float32)
        * inverse
    )
    fresh_masked = jnp.where(causal[None, None], fresh_raw, floor_score)
    fresh_top = jnp.max(fresh_masked, axis=3)
    fresh_expo = jnp.where(causal[None, None], jnp.exp(fresh_masked - fresh_top[..., None]), 0.0)
    fresh_total = jnp.sum(fresh_expo, axis=3)
    fresh_weights = fresh_expo.astype(jnp.bfloat16)
    fresh = jnp.einsum(
        "chrs,cshd->crhd", fresh_weights, fresh_values, preferred_element_type=jnp.float32
    )
    fresh = fresh / jnp.transpose(fresh_total, (0, 2, 1))[..., None]
    fresh = fresh.reshape(row_count, heads_here, head_width)
    fresh_lse = jnp.transpose(fresh_top + jnp.log(fresh_total), (1, 0, 2)).reshape(
        heads_here, row_count
    )
    home_parts, home_lses = (
        lax.all_to_all(parts.astype(jnp.float32), "ctx", split_axis=0, concat_axis=0, tiled=True),
        lax.all_to_all(lses, "ctx", split_axis=0, concat_axis=0, tiled=True),
    )
    peak = jnp.maximum(jnp.max(home_lses, axis=0), fresh_lse)
    block_weight = jnp.exp(home_lses - peak[None])
    fresh_weight = jnp.exp(fresh_lse - peak)
    numer_all = jnp.transpose(fresh_weight)[:, :, None] * fresh
    numer_all = numer_all + jnp.sum(
        jnp.transpose(block_weight, (0, 2, 1))[..., None] * home_parts, axis=0
    )
    denom_all = fresh_weight + jnp.sum(block_weight, axis=0)
    attended = (numer_all / jnp.transpose(denom_all)[:, :, None]).astype(jnp.bfloat16)
    flat = attended.reshape(row_count, heads_here * head_width)
    return project_and_reduce(flat, out_weight)


def solution(mesh):
    placed = (
        P("ctx", "head", None),
        P(None, "ctx", None),
        P(None, "ctx", None),
        P(None, "ctx"),
        P(),
        P("ctx"),
        P(),
        P("ctx", None, None),
        P("ctx", None, None),
        P("head"),
        P("head", None),
    )
    return jax.shard_map(
        shards, mesh=mesh, in_specs=placed, out_specs=P("ctx", "head"), check_vma=False
    )
```
